128 devices in a mesh: dp: 8 (over y, core), ctx: 16 (over x, z).
Axes of the slice: x: 4, y: 4, z: 4, core: 2. Of those that a mesh axis runs over, the one named last changes fastest.
Arguments:
- normed: bfloat16 [8, 2048, 8192], P('dp', 'ctx'), may hold values from -6 to 6
- queries: bfloat16 [8, 2048, 4096], P('dp', 'ctx'), may hold values from -4.5 to 4.5
- rotated_keys: bfloat16 [8, 2048, 512], P('dp', 'ctx'), may hold values from -4.5 to 4.5
- value_weight: bfloat16 [8192, 512], replicated, may hold values from -0.0625 to 0.0625
- adapter_down: bfloat16 [8192, 64], replicated, may hold values from -0.0625 to 0.0625
- adapter_up: bfloat16 [64, 512], replicated, may hold values from -0.75 to 0.75
- attention_cotangent: bfloat16 [8, 2048, 4096], P('dp', 'ctx'), may hold values from -6 to 6
- document_index: int32 [8, 2048], P('dp', 'ctx'), may hold values from 0 to 3, never falling along the last dimension, each value on 1 to 1024 neighbouring positions
- owner_routing: int32 [8, 2048, 1], P('dp', 'ctx'), may hold values from 0 to 15; in each aligned block of 128 rows (0 to 127, 128 to 255, ..., all dimensions but the last counted through in order) at most 12 rows name the same one
Outputs:
- attention_output: bfloat16 [8, 2048, 4096], P('dp', 'ctx')
- query_gradient: bfloat16 [8, 2048, 4096], P('dp', 'ctx')
- d_key: bfloat16 [8, 2048, 512], P('dp', 'ctx')
- normed_input_gradient: bfloat16 [8, 2048, 8192], P('dp', 'ctx')
- down_factor_gradient: float32 [8192, 64], replicated
- up_factor_gradient: float32 [64, 512], replicated
- row_logsumexp: float32 [8, 3072, 32], P('dp', 'ctx')
The draws below stay inside these ranges and needn't reach their ends.
Inputs may be any that keep to these rules, and one draw needn't show every extreme that they name: `document_index`: along a window the numbers never fall; each document covers 1 to 1024 positions, and one covers exactly 1024. `owner_routing`: among the 128 tokens of one device no owner is named by more than 12 tokens, a bound that some block reaches.
All inputs are finite; a program needn't handle non-finite values.
Results may differ from the reference program's by a relative error of at most 0.023.
Values may be sent and summed in bfloat16 or wider, within the bound.
No kernel may reach another device: no remote copies, remote signals or barrier semaphores. Data moves between devices by JAX's collectives and lax.ppermute only.
A program may use at most 192 MiB of HBM per device.

```python
import math
import jax
import jax.numpy as jnp
import numpy as np
from jax import lax

MODEL_WIDTH = 8192
HEAD_SIZE = 128
HQ = 32
KEY_HEADS = 4
ADAPTER_RANK = 64
TOK_DEV = 128
OWNERS = 16
PACKED_BATCH = 8
WINDOW_TOKENS = 2048
CAP = 12
SLOTS = 3072
NDOC = 4
MOST_DOC = 1024


def draw_queries(key, part):
    key = jax.random.fold_in(key, 1)
    result = jnp.clip(jax.random.normal(key, (PACKED_BATCH, WINDOW_TOKENS, HQ * HEAD_SIZE), jnp.float32), -4.0, 4.0)
    return result.astype(jnp.bfloat16)


def draw_rotated_keys(key, part):
    key = jax.random.fold_in(key, 2)
    result = jnp.clip(jax.random.normal(key, (PACKED_BATCH, WINDOW_TOKENS, KEY_HEADS * HEAD_SIZE), jnp.float32), -4.0, 4.0)
    return result.astype(jnp.bfloat16)


def steps_of(key, extent, pieces, low, largest):
    loudness, own = 1.0, jax.random.fold_in(key, 6)
    for position, blocks in pieces:
        steps = jnp.exp(jax.random.uniform(jax.random.fold_in(own, position), (blocks,), jnp.float32, low / len(pieces), largest / len(pieces)))
        loudness = loudness * jnp.repeat(steps, extent[position] // blocks).reshape([-1 if axis == position else 1 for axis in range(len(extent))])
    return loudness


def split_up(number_of, total, bound, skew):
    loads = [(1 << 20) // math.isqrt(rank ** skew) + 1 for rank in range(2, number_of + 1)]
    spare, holding = total - bound - (number_of - 1), [1] * (number_of - 1)
    while spare > 0:
        movable = [i for i in range(number_of - 1) if holding[i] < bound]
        pool, left = sum([loads[i] for i in movable]), spare
        for i in movable:
            more = min(bound - holding[i], max(1, left * loads[i] // pool), spare)
            holding[i] = holding[i] + more
            spare = spare - more
    return np.array([bound] + holding)


def ragged(own_key, amount, total, bound, lean):
    if amount == 2:
        one = jax.random.randint(own_key, (), max(1, total - bound), min(bound, total - 1) + 1)
        return jnp.stack([one, total - one])
    tallies = jnp.asarray(split_up(amount, total, bound, lean), jnp.int32)
    couples = (amount - 1) // 2
    giver, receiver = tallies[1:1 + 2 * couples:2], tallies[2:2 + 2 * couples:2]
    room = jnp.minimum(giver - 1, bound - receiver)
    passed = jax.random.randint(jax.random.fold_in(own_key, 1), (couples,), 0, 1 << 20) % (room + 1)
    tallies = tallies.at[1:1 + 2 * couples:2].set(giver - passed).at[2:2 + 2 * couples:2].set(receiver + passed)
    return tallies[jax.random.permutation(jax.random.fold_in(own_key, 2), amount)]


def deal_out(own_key, own, number, rows, number_of, top, limit, skew):
    order = jax.random.permutation(own_key, number_of)
    crowded, usual = shares(number_of, rows * top, limit, skew, True), shares(number_of, rows * top, limit, skew, False)
    places = jnp.arange(number_of)

    def named(lengths, rotation):
        used = int((lengths > 0).sum())
        fixed = max(1, used // 4)
        shifted = fixed + (places - fixed + rotation * (used - fixed)) % max(1, number_of - fixed)
        return jnp.zeros((number_of,), jnp.int32).at[order[jnp.where(places < fixed, places, shifted)]].set(jnp.asarray(lengths, jnp.int32))

    lengths = jnp.where(number % 4 == 0, named(crowded, number // 4), named(usual, number - number // 4 - 1))
    mixed = jax.random.permutation(jax.random.fold_in(own, 3), number_of)
    giver, sink = mixed[0:number_of // 2 * 2:2], mixed[1:number_of // 2 * 2:2]
    room = jnp.minimum(lengths[giver] - 1, limit - lengths[sink]) // 2
    room = jnp.where((giver == order[0]) | (sink == order[0]) | (lengths[sink] == 0), 0, jnp.maximum(room, 0))
    shifted = jax.random.randint(jax.random.fold_in(own, 4), (number_of // 2,), 0, 1 << 20) % (room + 1)
    lengths = lengths.at[giver].add(-shifted).at[sink].add(shifted)
    labels = jnp.searchsorted(jnp.cumsum(lengths), jnp.arange(rows * top), side="right").astype(jnp.int32)
    table = labels.reshape(top, rows).T
    table = table[jax.random.permutation(jax.random.fold_in(own, 1), rows)]
    rotation = jax.random.randint(jax.random.fold_in(own, 2), (rows, 1), 0, top)
    return jnp.take_along_axis(table, (jnp.arange(top)[None, :] + rotation) % top, axis=1)


def shares(number_of, total, limit, slope, full):
    weights = [(1 << 20) // math.isqrt(grade ** slope) + 1 for grade in range(1, number_of + 1)]
    largest = limit if full else min(limit, max(-(-total // number_of), total * weights[0] // sum(weights)))
    least = 1 if total - largest >= number_of - 1 else 0
    given, rest = [largest] + [least] * (number_of - 1), total - largest - least * (number_of - 1)
    while rest > 0:
        candidates = [i for i in range(1, number_of) if given[i] < largest] or [i for i in range(1, number_of) if given[i] < limit]
        whole, budget = sum([weights[i] for i in candidates]), rest
        for i in candidates:
            more = min(limit - given[i], max(1, budget * weights[i] // whole), rest)
            given[i] = given[i] + more
            rest = rest - more
    return np.array(given)


def gaussian(own_key, extent, spread, limit, split=(), kind=jnp.bfloat16):
    entries = spread * jax.random.normal(own_key, extent, jnp.float32)
    if split:
        entries = entries * steps_of(own_key, extent, split, -0.22, 0.18)
    return jnp.clip(entries, -limit, limit).astype(kind)


def setup_inputs(seed: int = 0) -> dict:
    splits = jax.random.split(jax.random.key(seed), 10)
    normed = gaussian(splits[0], (PACKED_BATCH, WINDOW_TOKENS, MODEL_WIDTH), 1.0, 6.0, ((0, 8), (1, 16)))
    queries = draw_queries(jax.random.fold_in(splits[9], 71), 0)
    rotated_keys = draw_rotated_keys(jax.random.fold_in(splits[9], 71), 0)
    value_weight = gaussian(splits[3], (MODEL_WIDTH, KEY_HEADS * HEAD_SIZE), MODEL_WIDTH ** -0.5, 0.0625)
    adapter_down = gaussian(splits[4], (MODEL_WIDTH, ADAPTER_RANK), MODEL_WIDTH ** -0.5, 0.0625)
    adapter_up = gaussian(splits[5], (ADAPTER_RANK, KEY_HEADS * HEAD_SIZE), ADAPTER_RANK ** -0.5, 0.75)
    attention_cotangent = gaussian(splits[6], (PACKED_BATCH, WINDOW_TOKENS, HQ * HEAD_SIZE), 1.0, 6.0, ((0, 8), (1, 16)))
    document_index = jax.vmap(lambda own: jnp.searchsorted(jnp.cumsum(ragged(own, NDOC, WINDOW_TOKENS, MOST_DOC, 2)), jnp.arange(WINDOW_TOKENS), side="right"))(jax.random.split(splits[7], PACKED_BATCH)).reshape((PACKED_BATCH, WINDOW_TOKENS)).astype(jnp.int32)
    owner_routing_keys = jax.random.split(jax.random.fold_in(splits[8], 1), PACKED_BATCH * WINDOW_TOKENS // TOK_DEV)
    owner_routing_turns = jax.random.permutation(jax.random.fold_in(splits[8], 3), PACKED_BATCH * WINDOW_TOKENS // TOK_DEV)
    owner_routing = jax.vmap(lambda own, number: deal_out(jax.random.fold_in(splits[8], 2), own, number, TOK_DEV, OWNERS, 1, CAP, 1))(owner_routing_keys, owner_routing_turns).reshape((PACKED_BATCH, WINDOW_TOKENS, 1))
    return dict(normed=normed, queries=queries, rotated_keys=rotated_keys, value_weight=value_weight, adapter_down=adapter_down, adapter_up=adapter_up, attention_cotangent=attention_cotangent, document_index=document_index, owner_routing=owner_routing)


ADAPTER_SCALE = 0.5
NEG_FILL = -1e+30

def group_terms(query_group, key_group, value_group, grad_group, allowed):
    inv_root = 1.0 / math.sqrt(HEAD_SIZE)
    query_f32 = query_group.astype(jnp.float32)
    key_f32 = key_group.astype(jnp.float32)
    value_f32 = value_group.astype(jnp.float32)
    grad_f32 = grad_group.astype(jnp.float32)
    scores = jnp.einsum('qjd,kd->jqk', query_f32, key_f32) * inv_root
    row_peak = lax.optimization_barrier(jnp.max(jnp.where(allowed, scores, NEG_FILL), axis=-1))
    row_total = lax.optimization_barrier(jnp.sum(jnp.where(allowed, jnp.exp(scores - row_peak[..., None]), 0.0), axis=-1))
    row_logsumexp = row_peak + jnp.log(row_total)
    weights32 = jnp.where(allowed, jnp.exp(scores - row_logsumexp[..., None]), 0.0)
    weights = weights32.astype(jnp.bfloat16)
    outputs = jnp.einsum('jqk,kd->qjd', weights.astype(jnp.float32), value_f32).astype(jnp.bfloat16)
    row_delta = lax.optimization_barrier(jnp.sum(grad_f32 * outputs.astype(jnp.float32), axis=-1))
    d_prob = jnp.einsum('qjd,kd->jqk', grad_f32, value_f32)
    d_scores = (weights32 * (d_prob - row_delta.T[..., None])).astype(jnp.bfloat16)
    d_query = (jnp.einsum('jqk,kd->qjd', d_scores.astype(jnp.float32), key_f32) * inv_root).astype(jnp.bfloat16)
    key_gradient = jnp.einsum('jqk,qjd->kd', d_scores.astype(jnp.float32), query_f32) * inv_root
    d_values = jnp.einsum('jqk,qjd->kd', weights.astype(jnp.float32), grad_f32)
    return (outputs, row_logsumexp, d_query, key_gradient, d_values)

def window_terms(inputs):
    query_w, key_w, value_w, grad_w, seg_w = inputs
    seq_len = query_w.shape[0]
    per_group = HQ // KEY_HEADS
    spots = jnp.arange(seq_len, dtype=jnp.int32)
    allowed = (seg_w[:, None] == seg_w[None, :]) & (spots[None, :] <= spots[:, None])
    query_groups = query_w.reshape(seq_len, KEY_HEADS, per_group, HEAD_SIZE).transpose(1, 0, 2, 3)
    key_groups = key_w.reshape(seq_len, KEY_HEADS, HEAD_SIZE).transpose(1, 0, 2)
    value_groups = value_w.reshape(seq_len, KEY_HEADS, HEAD_SIZE).transpose(1, 0, 2)
    grad_groups = grad_w.reshape(seq_len, KEY_HEADS, per_group, HEAD_SIZE).transpose(1, 0, 2, 3)
    outputs, row_logsumexp, d_query, key_gradient, d_values = lax.map(lambda parts: group_terms(parts[0], parts[1], parts[2], parts[3], allowed), (query_groups, key_groups, value_groups, grad_groups))
    outputs = outputs.transpose(1, 0, 2, 3).reshape(seq_len, HQ * HEAD_SIZE)
    row_logsumexp = row_logsumexp.transpose(2, 0, 1).reshape(seq_len, HQ)
    d_query = d_query.transpose(1, 0, 2, 3).reshape(seq_len, HQ * HEAD_SIZE)
    key_gradient = key_gradient.transpose(1, 0, 2).reshape(seq_len, KEY_HEADS * HEAD_SIZE)
    d_values = d_values.transpose(1, 0, 2).reshape(seq_len, KEY_HEADS * HEAD_SIZE)
    return (outputs, row_logsumexp, d_query, key_gradient, d_values)

def slot_of_tokens(plan_w):
    owners = plan_w[:, 0]
    onehot = (owners[:, None] == jnp.arange(OWNERS, dtype=jnp.int32)[None, :]).astype(jnp.int32)
    blocks = onehot.reshape(OWNERS, TOK_DEV, OWNERS)
    earlier = jnp.cumsum(blocks, axis=1) - blocks
    slot_rank = lax.optimization_barrier(jnp.sum(earlier * blocks, axis=-1)).reshape(-1)
    source = jnp.arange(WINDOW_TOKENS, dtype=jnp.int32) // TOK_DEV
    return owners * (OWNERS * CAP) + source * CAP + slot_rank

def place_lse(lse_w, plan_w):
    return jnp.zeros((SLOTS, HQ), jnp.float32).at[slot_of_tokens(plan_w)].set(lse_w)

def reference(normed, queries, rotated_keys, value_weight, adapter_down, adapter_up, attention_cotangent, document_index, owner_routing):
    flattened_rows = normed.reshape(-1, MODEL_WIDTH)
    adapter_product = jnp.dot(flattened_rows, adapter_down, preferred_element_type=jnp.float32).astype(jnp.bfloat16)
    value_rows = (jnp.dot(flattened_rows, value_weight, preferred_element_type=jnp.float32) + ADAPTER_SCALE * jnp.dot(adapter_product, adapter_up, preferred_element_type=jnp.float32)).astype(jnp.bfloat16)
    value_w = value_rows.reshape(PACKED_BATCH, WINDOW_TOKENS, KEY_HEADS * HEAD_SIZE)
    attention_output, lse, query_gradient, key_gradient, d_values = lax.map(window_terms, (queries, rotated_keys, value_w, attention_cotangent, document_index))
    row_logsumexp = jax.vmap(place_lse)(lse, owner_routing)
    value_gradient = d_values.reshape(-1, KEY_HEADS * HEAD_SIZE).astype(jnp.bfloat16)
    adapter_middle = (ADAPTER_SCALE * jnp.dot(value_gradient, adapter_up.T, preferred_element_type=jnp.float32)).astype(jnp.bfloat16)
    normed_input_gradient = (jnp.dot(value_gradient, value_weight.T, preferred_element_type=jnp.float32) + jnp.dot(adapter_middle, adapter_down.T, preferred_element_type=jnp.float32)).astype(jnp.bfloat16)
    down_factor_gradient = jnp.dot(flattened_rows.T, adapter_middle, preferred_element_type=jnp.float32)
    up_factor_gradient = ADAPTER_SCALE * jnp.dot(adapter_product.T, value_gradient, preferred_element_type=jnp.float32)
    return (attention_output, query_gradient, key_gradient.astype(jnp.bfloat16), normed_input_gradient.reshape(PACKED_BATCH, WINDOW_TOKENS, MODEL_WIDTH), down_factor_gradient, up_factor_gradient, row_logsumexp)
```

```python
import functools
import math

import jax
import jax.numpy as jnp
from jax import lax
from jax.experimental import pallas as pl
from jax.experimental.pallas import tpu as pltpu
from jax.sharding import PartitionSpec as P

HEAD = 128
HQ = 32
GROUPS = 4
PER_GROUP = HQ // GROUPS
PAIRS = PER_GROUP // 2
CAP = 12
TOK = 128
REACH = 8
BLOCKS = REACH + 1
KEYS = BLOCKS * TOK
DOC_ROWS = 16
PACK = TOK + DOC_ROWS
KV = GROUPS * HEAD
ADAPTER_SCALE = 0.5
INV_ROOT = 1.0 / math.sqrt(HEAD)
LOG2E = 1.4426950408889634
LN2 = 0.6931471805599453
MASKED = -1e30
VMEM = 56 << 20
BF = jnp.bfloat16
F32 = jnp.float32
NT = (((1,), (1,)), ((), ()))
NN = (((1,), (0,)), ((), ()))


def dot(a, b, dims=NN):
    return lax.dot_general(a, b, dims, preferred_element_type=F32)


def window_part(own, pairs, distance):
    if distance % 4 == 0:
        return own[distance // 4]
    return pairs[distance % 4 - 1].at[distance // 4]


def fill_bias(here, parts, docs_own, bias):
    own = docs_own.astype(F32)
    real = [jnp.where(here - REACH + k >= 0, 1.0, 0.0) for k in range(BLOCKS)]
    docs = [parts[k][pl.ds(TOK, DOC_ROWS), :].astype(F32) for k in range(BLOCKS)]
    missing = jnp.maximum(REACH - here, 0) * TOK
    start = jnp.zeros((1, TOK), F32)
    for number in (1, 2, 3):
        lower = jnp.zeros((DOC_ROWS, TOK), F32)
        for k in range(BLOCKS):
            lower = lower + jnp.where(docs[k] < number, real[k], 0.0)
        start = jnp.where(own == number, jnp.sum(lower) / DOC_ROWS, start)
    first = start.astype(jnp.int32) + missing
    lane = lax.broadcasted_iota(jnp.int32, (TOK, TOK), 1)
    row = lax.broadcasted_iota(jnp.int32, (TOK, TOK), 0)
    for k in range(BLOCKS):
        spot = row + k * TOK
        seen = (spot >= first) & (spot <= REACH * TOK + lane)
        bias[pl.ds(k * TOK, TOK), :] = jnp.where(seen, 0.0, MASKED)


def pair_rows(ref, pair):
    return jnp.concatenate(
        [ref[:, (2 * pair + n) * HEAD : (2 * pair + n + 1) * HEAD] for n in range(2)], axis=0
    )


def block(k):
    return pl.ds(k * TOK, TOK)


def fold(x, op):
    return op(x.reshape(TOK // 8, 8, 2 * TOK), axis=0)


def scores_kernel(here_ref, docs_ref, owners_ref, q_ref, g_ref, *rest):
    key_own, key_pairs = rest[:3], rest[3:6]
    lse_ref, slots_ref, *outs = rest[6:12]
    bias, scores, weights, lse_all = rest[12:]
    group = pl.program_id(0)
    here = here_ref[0]
    parts = [window_part(key_own, key_pairs, REACH - k) for k in range(BLOCKS)]

    @pl.when(group == 0)
    def _():
        fill_bias(here, parts, docs_ref[...], bias)

    keys = [part[pl.ds(0, TOK), :] for part in parts]
    for pair in range(PAIRS):
        q2 = pair_rows(q_ref, pair)
        peak = jnp.full((8, 2 * TOK), MASKED, F32)
        for k in range(BLOCKS):
            b = bias[block(k), :]
            t = dot(keys[k], q2, NT) * (INV_ROOT * LOG2E) + jnp.concatenate(
                [b, b], axis=1
            )
            scores[block(k), :] = t
            peak = jnp.maximum(peak, fold(t, jnp.max))
        peak = jnp.max(peak, axis=0, keepdims=True)
        total = jnp.zeros((8, 2 * TOK), F32)
        for k in range(BLOCKS):
            total = total + fold(jnp.exp2(scores[block(k), :] - peak), jnp.sum)
        lse2 = peak + jnp.log2(jnp.sum(total, axis=0, keepdims=True))
        for n in range(2):
            lse = lse2[:, n * TOK : (n + 1) * TOK] * LN2
            lse_ref[0, 2 * pair + n : 2 * pair + n + 1, :] = lse
            lse_all[pl.ds(group * PER_GROUP + 2 * pair + n, 1), :] = lse
        for k in range(BLOCKS):
            weights[block(k), pl.ds(pair * 2 * TOK, 2 * TOK)] = jnp.exp2(
                scores[block(k), :] - lse2
            ).astype(BF)
    rows = jnp.concatenate([pair_rows(g_ref, pair) for pair in range(PAIRS)], axis=0)
    for k in range(BLOCKS):
        put_partial(outs, REACH - k, dot(weights[block(k), :], rows).astype(BF))

    @pl.when(group == GROUPS - 1)
    def _():
        put_slots(owners_ref[...], lse_all[...], slots_ref)


def put_slots(owners, lse, slots_ref):
    peers = slots_ref.shape[0]
    named = lax.broadcasted_iota(jnp.int32, (peers, TOK), 0) == owners
    onehot = jnp.where(named, 1.0, 0.0)
    before = lax.broadcasted_iota(jnp.int32, (TOK, TOK), 0) < lax.broadcasted_iota(
        jnp.int32, (TOK, TOK), 1
    )
    earlier = dot(onehot.astype(BF), jnp.where(before, 1.0, 0.0).astype(BF))
    for slot in range(CAP):
        place = jnp.where(named & (earlier == slot), 1.0, 0.0)
        slots_ref[:, slot * HQ : (slot + 1) * HQ] = lax.dot_general(
            place, lse, NT, precision=lax.Precision.HIGHEST, preferred_element_type=F32
        )


def put_partial(outs, distance, value):
    if distance % 4 == 0:
        outs[0][distance // 4] = value
    else:
        outs[4 - distance % 4][distance // 4] = value


def grads_kernel(here_ref, docs_ref, q_ref, g_ref, lse_ref, *rest):
    key_own, key_pairs, value_own, value_pairs = rest[:3], rest[3:6], rest[6:9], rest[9:12]
    out_ref, dq_ref, *outs = rest[12:18]
    bias, keys_t, values_t, weights32, weights, d_scores = rest[18:]
    group = pl.program_id(0)
    here = here_ref[0]
    parts = [window_part(key_own, key_pairs, REACH - k) for k in range(BLOCKS)]

    @pl.when(group == 0)
    def _():
        fill_bias(here, parts, docs_ref[...], bias)

    keys = [part[pl.ds(0, TOK), :] for part in parts]
    values = [window_part(value_own, value_pairs, REACH - k)[...] for k in range(BLOCKS)]
    for k in range(BLOCKS):
        keys_t[:, block(k)] = keys[k].astype(F32).T.astype(BF)
        values_t[:, block(k)] = values[k].astype(F32).T.astype(BF)
    for pair in range(PAIRS):
        q2 = pair_rows(q_ref, pair)
        g2 = pair_rows(g_ref, pair)
        lse2 = (
            jnp.concatenate(
                [lse_ref[0, 2 * pair + n : 2 * pair + n + 1, :] for n in range(2)], axis=1
            )
            * LOG2E
        )
        for k in range(BLOCKS):
            b = bias[block(k), :]
            t = dot(keys[k], q2, NT) * (INV_ROOT * LOG2E) + jnp.concatenate(
                [b, b], axis=1
            )
            w = jnp.exp2(t - lse2)
            weights32[block(k), :] = w
            weights[block(k), :] = w.astype(BF)
        out_t = dot(values_t[...], weights[...]).astype(BF).astype(F32)
        g2_t = jnp.concatenate(
            [g2[n * TOK : (n + 1) * TOK].astype(F32).T for n in range(2)], axis=1
        )
        delta = jnp.sum(out_t * g2_t, axis=0, keepdims=True)
        for k in range(BLOCKS):
            d_prob = dot(values[k], g2, NT)
            d_scores[block(k), pl.ds(pair * 2 * TOK, 2 * TOK)] = (
                weights32[block(k), :] * (d_prob - delta)
            ).astype(BF)
        dq_t = dot(keys_t[...], d_scores[:, pl.ds(pair * 2 * TOK, 2 * TOK)]) * INV_ROOT
        for n in range(2):
            head = slice((2 * pair + n) * HEAD, (2 * pair + n + 1) * HEAD)
            out_ref[:, head] = out_t[:, n * TOK : (n + 1) * TOK].T.astype(BF)
            dq_ref[:, head] = dq_t[:, n * TOK : (n + 1) * TOK].T.astype(BF)
    rows = jnp.concatenate([pair_rows(q_ref, pair) for pair in range(PAIRS)], axis=0)
    for k in range(BLOCKS):
        put_partial(
            outs, REACH - k, (dot(d_scores[block(k), :], rows) * INV_ROOT).astype(BF)
        )


def smem():
    return pl.BlockSpec(memory_space=pltpu.SMEM)


def partial_outs():
    shapes = [jax.ShapeDtypeStruct((n, TOK, KV), BF) for n in (3, 2, 2, 2)]
    specs = [pl.BlockSpec((n, TOK, HEAD), lambda g: (0, 0, g)) for n in (3, 2, 2, 2)]
    return shapes, specs


def part_specs(rows):
    own = pl.BlockSpec((rows, HEAD), lambda g: (0, g))
    pair = pl.BlockSpec((2, rows, HEAD), lambda g: (0, 0, g))
    return [own] * 3 + [pair] * 3


def run_scores(here, docs_own, owners, queries, grads, keys):
    shapes, specs = partial_outs()
    wide = pl.BlockSpec((TOK, PER_GROUP * HEAD), lambda g: (0, g))
    line = pl.BlockSpec((1, TOK), lambda g: (0, 0))
    return pl.pallas_call(
        scores_kernel,
        grid=(GROUPS,),
        in_specs=[smem(), line, line, wide, wide] + part_specs(PACK),
        out_specs=[
            pl.BlockSpec((1, PER_GROUP, TOK), lambda g: (g, 0, 0)),
            pl.BlockSpec((16, CAP * HQ), lambda g: (0, 0)),
        ]
        + specs,
        out_shape=[
            jax.ShapeDtypeStruct((GROUPS, PER_GROUP, TOK), F32),
            jax.ShapeDtypeStruct((16, CAP * HQ), F32),
        ]
        + shapes,
        scratch_shapes=[
            pltpu.VMEM((KEYS, TOK), F32),
            pltpu.VMEM((KEYS, 2 * TOK), F32),
            pltpu.VMEM((KEYS, PER_GROUP * TOK), BF),
            pltpu.VMEM((HQ, TOK), F32),
        ],
        compiler_params=pltpu.CompilerParams(
            vmem_limit_bytes=VMEM, dimension_semantics=("arbitrary",)
        ),
        cost_estimate=pl.CostEstimate(
            flops=2 * 2 * HQ * TOK * KEYS * HEAD, bytes_accessed=6 << 20, transcendentals=2 * HQ * TOK * KEYS
        ),
        name="scores",
    )(here, docs_own, owners, queries, grads, *keys)


def run_grads(here, docs_own, queries, grads, lse, keys, values):
    shapes, specs = partial_outs()
    wide = pl.BlockSpec((TOK, PER_GROUP * HEAD), lambda g: (0, g))
    return pl.pallas_call(
        grads_kernel,
        grid=(GROUPS,),
        in_specs=[
            smem(),
            pl.BlockSpec((1, TOK), lambda g: (0, 0)),
            wide,
            wide,
            pl.BlockSpec((1, PER_GROUP, TOK), lambda g: (g, 0, 0)),
        ]
        + part_specs(PACK)
        + part_specs(TOK),
        out_specs=[wide, wide] + specs,
        out_shape=[jax.ShapeDtypeStruct((TOK, HQ * HEAD), BF)] * 2 + shapes,
        scratch_shapes=[
            pltpu.VMEM((KEYS, TOK), F32),
            pltpu.VMEM((HEAD, KEYS), BF),
            pltpu.VMEM((HEAD, KEYS), BF),
            pltpu.VMEM((KEYS, 2 * TOK), F32),
            pltpu.VMEM((KEYS, 2 * TOK), BF),
            pltpu.VMEM((KEYS, PER_GROUP * TOK), BF),
        ],
        compiler_params=pltpu.CompilerParams(
            vmem_limit_bytes=VMEM, dimension_semantics=("arbitrary",)
        ),
        cost_estimate=pl.CostEstimate(
            flops=5 * 2 * HQ * TOK * KEYS * HEAD, bytes_accessed=8 << 20, transcendentals=HQ * TOK * KEYS
        ),
        name="grads",
    )(here, docs_own, queries, grads, lse, *keys, *values)


def along_z(x, step):
    return lax.ppermute(x, "ctx", [(i, i // 4 * 4 + (i + step) % 4) for i in range(16)])


def along_x(x, step):
    return lax.ppermute(x, "ctx", [(i, (i + 4 * step) % 16) for i in range(16)])


def along_y(x, step):
    return lax.ppermute(x, "dp", [(i, (i + 2 * step) % 8) for i in range(8)])


def other_core(x):
    return lax.ppermute(x, "dp", [(i, i ^ 1) for i in range(8)])


def from_rows(x):
    return [x, along_x(x, 1), along_x(x, 2)]


def from_peers(own, z):
    late = jnp.stack(own[1:])
    early = jnp.stack(own[:2])
    return [along_z(jnp.where(z + e > 3, late, early), e) for e in (1, 2, 3)]


def sum_of_four(x, move):
    near = move(x, 1).astype(F32) + move(x, 3).astype(F32)
    return ((x.astype(F32) + move(x, 2).astype(F32)) + near).astype(BF)


def collect(own, to_peer, z):
    here_row = own[0].astype(F32)
    row_1 = own[1].astype(F32)
    row_2 = own[2].astype(F32)
    for e in (1, 2, 3):
        got = along_z(to_peer[e - 1], e)
        near, far = got[0].astype(F32), got[1].astype(F32)
        wrapped = e > z
        here_row = here_row + jnp.where(wrapped, near, 0.0)
        row_1 = row_1 + jnp.where(wrapped, far, near)
        row_2 = row_2 + jnp.where(wrapped, 0.0, far)
    from_1 = along_x(row_1.astype(BF), -1)
    from_2 = along_x(row_2.astype(BF), -2)
    return here_row + from_1.astype(F32) + from_2.astype(F32)


def local(
    normed,
    queries,
    rotated_keys,
    value_weight,
    adapter_down,
    adapter_up,
    attention_cotangent,
    document_index,
    owner_routing,
):
    ctx = lax.axis_index("ctx")
    dp = lax.axis_index("dp")
    z, y, core = ctx % 4, dp // 2, dp % 2
    rows = normed[0]
    low_rank = dot(rows, adapter_down).astype(BF)
    values = (dot(rows, value_weight) + ADAPTER_SCALE * dot(low_rank, adapter_up)).astype(BF)
    doc_rows = jnp.broadcast_to(
        jnp.tile(document_index.astype(BF), (1, KV // TOK)), (DOC_ROWS, KV)
    )
    key_own = from_rows(jnp.concatenate([rotated_keys[0], doc_rows], axis=0))
    value_own = from_rows(values)
    key_parts = key_own + from_peers(key_own, z)
    value_parts = value_own + from_peers(value_own, z)
    here = ctx.reshape(1)
    lse, send_lse, *dv_parts = run_scores(
        here,
        document_index,
        owner_routing.reshape(1, TOK),
        queries[0],
        attention_cotangent[0],
        key_parts,
    )
    value_grad = collect(dv_parts[0], dv_parts[1:], z).astype(BF)
    out, dq, *dk_parts = run_grads(
        here, document_index, queries[0], attention_cotangent[0], lse, key_parts, value_parts
    )

    peers = lax.axis_size("ctx")
    lse_rows = lax.all_to_all(
        send_lse.reshape(peers, 1, CAP * HQ), "ctx", split_axis=0, concat_axis=0, tiled=True
    ).reshape(peers * CAP, HQ)

    middle = (ADAPTER_SCALE * dot(value_grad, adapter_up, NT)).astype(BF)
    tn = (((0,), (0,)), ((), ()))
    down_part = dot(middle, rows, tn).astype(BF)
    up_part = (ADAPTER_SCALE * dot(low_rank, value_grad, tn)).astype(BF)
    both = jnp.concatenate([down_part, up_part], axis=1)
    width = both.shape[1]
    half = both.shape[0] // 2
    keep = lax.dynamic_slice(both, (core * half, 0), (half, width))
    send = lax.dynamic_slice(both, ((1 - core) * half, 0), (half, width))
    summed = (keep.astype(F32) + other_core(send).astype(F32)).astype(BF)
    part = width // 4

    def quarter(x, n):
        return lax.dynamic_slice(x, (0, (n % 4) * part), (half, part))

    mine = quarter(summed, y).astype(F32)
    for e in (1, 2, 3):
        mine = mine + along_y(quarter(summed, y + e), e).astype(F32)
    mine = sum_of_four(sum_of_four(mine.astype(BF), along_x), along_z)
    whole = jnp.zeros((half, width), BF)
    for e in range(4):
        got = along_y(mine, e) if e else mine
        whole = lax.dynamic_update_slice(whole, got, (0, ((y - e) % 4) * part))
    other = other_core(whole)
    total = jnp.concatenate(
        [jnp.where(core == 0, whole, other), jnp.where(core == 0, other, whole)], axis=0
    ).astype(F32)
    model = rows.shape[1]
    total_down = total[:, :model].T
    total_up = total[:, model:]

    normed_input_gradient = (dot(value_grad, value_weight, NT) + dot(middle, adapter_down, NT)).astype(BF)
    d_key = collect(dk_parts[0], dk_parts[1:], z).astype(BF)
    return (
        out[None],
        dq[None],
        d_key[None],
        normed_input_gradient[None],
        total_down,
        total_up,
        lse_rows[None],
    )


def solution(mesh):
    tokens = P("dp", "ctx", None)
    return jax.shard_map(
        local,
        mesh=mesh,
        in_specs=(tokens, tokens, tokens, P(), P(), P(), tokens, P("dp", "ctx"), tokens),
        out_specs=(tokens, tokens, tokens, tokens, P(), P(), tokens),
        check_vma=False,
    )
```

```python
import functools
import math

import jax
import jax.numpy as jnp
from jax import lax
from jax.experimental import pallas as pl
from jax.experimental.pallas import tpu as pltpu
from jax.sharding import PartitionSpec as P

HEAD = 128
HQ = 32
GROUPS = 4
PER_GROUP = HQ // GROUPS
PAIRS = PER_GROUP // 2
CAP = 12
TOK = 128
REACH = 8
BLOCKS = REACH + 1
KEYS = BLOCKS * TOK
DOC_ROWS = 16
PACK = TOK + DOC_ROWS
KV = GROUPS * HEAD
ADAPTER_SCALE = 0.5
INV_ROOT = 1.0 / math.sqrt(HEAD)
LOG2E = 1.4426950408889634
LN2 = 0.6931471805599453
MASKED = -1e30
VMEM = 56 << 20
SMALL_VMEM = 20 << 20
BF = jnp.bfloat16
F32 = jnp.float32
NT = (((1,), (1,)), ((), ()))
NN = (((1,), (0,)), ((), ()))


def dot(a, b, dims=NN):
    return lax.dot_general(a, b, dims, preferred_element_type=F32)


def window_part(own, pairs, distance):
    if distance % 4 == 0:
        return own[distance // 4]
    return pairs[distance % 4 - 1].at[distance // 4]


def put_partials(outs, value_of):
    for distance in range(BLOCKS):
        outs[-distance % 4][distance // 4] = value_of(REACH - distance)


def fill_bias(here, parts, docs_own, bias):
    own = docs_own.astype(F32)
    real = [jnp.where(here - REACH + k >= 0, 1.0, 0.0) for k in range(BLOCKS)]
    docs = [parts[k][pl.ds(TOK, DOC_ROWS), :].astype(F32) for k in range(BLOCKS)]
    missing = jnp.maximum(REACH - here, 0) * TOK
    start = jnp.zeros((1, TOK), F32)
    for number in (1, 2, 3):
        lower = jnp.zeros((DOC_ROWS, TOK), F32)
        for k in range(BLOCKS):
            lower = lower + jnp.where(docs[k] < number, real[k], 0.0)
        start = jnp.where(own == number, jnp.sum(lower) / DOC_ROWS, start)
    first = start.astype(jnp.int32) + missing
    lane = lax.broadcasted_iota(jnp.int32, (TOK, TOK), 1)
    row = lax.broadcasted_iota(jnp.int32, (TOK, TOK), 0)
    for k in range(BLOCKS):
        spot = row + k * TOK
        seen = (spot >= first) & (spot <= REACH * TOK + lane)
        bias[pl.ds(k * TOK, TOK), :] = jnp.where(seen, 0.0, MASKED)


def pair_rows(ref, pair):
    return jnp.concatenate(
        [ref[:, (2 * pair + n) * HEAD : (2 * pair + n + 1) * HEAD] for n in range(2)], axis=0
    )


def block(k):
    return pl.ds(k * TOK, TOK)


def fold(x, op):
    return op(x.reshape(TOK // 8, 8, 2 * TOK), axis=0)


def scores_kernel(here_ref, docs_ref, owners_ref, q_ref, g_ref, *rest):
    key_own, key_pairs = rest[:3], rest[3:6]
    lse_ref, slots_ref, *dv_refs = rest[7:13]
    bias, scores, weights, lse_all = rest[13:]
    parts = [window_part(key_own, key_pairs, REACH - k) for k in range(BLOCKS)]
    group = pl.program_id(0)
    here = here_ref[0]

    @pl.when(group == 0)
    def _():
        fill_bias(here, parts, docs_ref[...], bias)

    keys = [part[pl.ds(0, TOK), :] for part in parts]
    for pair in range(PAIRS):
        q2 = pair_rows(q_ref, pair)
        peak = jnp.full((8, 2 * TOK), MASKED, F32)
        for k in range(BLOCKS):
            b = bias[block(k), :]
            t = dot(keys[k], q2, NT) * (INV_ROOT * LOG2E) + jnp.concatenate(
                [b, b], axis=1
            )
            scores[block(k), :] = t
            peak = jnp.maximum(peak, fold(t, jnp.max))
        peak = jnp.max(peak, axis=0, keepdims=True)
        total = jnp.zeros((8, 2 * TOK), F32)
        for k in range(BLOCKS):
            total = total + fold(jnp.exp2(scores[block(k), :] - peak), jnp.sum)
        lse2 = peak + jnp.log2(jnp.sum(total, axis=0, keepdims=True))
        for n in range(2):
            lse = lse2[:, n * TOK : (n + 1) * TOK] * LN2
            lse_ref[0, 2 * pair + n : 2 * pair + n + 1, :] = lse
            lse_all[pl.ds(group * PER_GROUP + 2 * pair + n, 1), :] = lse
        for k in range(BLOCKS):
            weights[block(k), pl.ds(pair * 2 * TOK, 2 * TOK)] = jnp.exp2(
                scores[block(k), :] - lse2
            ).astype(BF)
    rows = jnp.concatenate([pair_rows(g_ref, pair) for pair in range(PAIRS)], axis=0)
    put_partials(dv_refs, lambda k: dot(weights[block(k), :], rows).astype(BF))

    @pl.when(group == GROUPS - 1)
    def _():
        put_slots(owners_ref[...], lse_all[...], slots_ref)


def put_slots(owners, lse, slots_ref):
    peers = slots_ref.shape[0]
    named = lax.broadcasted_iota(jnp.int32, (peers, TOK), 0) == owners
    onehot = jnp.where(named, 1.0, 0.0)
    before = lax.broadcasted_iota(jnp.int32, (TOK, TOK), 0) < lax.broadcasted_iota(
        jnp.int32, (TOK, TOK), 1
    )
    earlier = dot(onehot.astype(BF), jnp.where(before, 1.0, 0.0).astype(BF))
    for slot in range(CAP):
        place = jnp.where(named & (earlier == slot), 1.0, 0.0)
        slots_ref[:, 0, slot * HQ : (slot + 1) * HQ] = lax.dot_general(
            place, lse, NT, precision=lax.Precision.HIGHEST, preferred_element_type=F32
        )


def grads_kernel(here_ref, docs_ref, q_ref, g_ref, lse_ref, *rest):
    key_own, key_pairs, value_own, value_pairs = rest[:3], rest[3:6], rest[6:9], rest[9:12]
    out_ref, dq_ref, *dk_refs = rest[12:18]
    bias, keys_t, values_t, weights32, weights, d_scores = rest[18:]
    parts = [window_part(key_own, key_pairs, REACH - k) for k in range(BLOCKS)]
    group = pl.program_id(0)
    here = here_ref[0]

    @pl.when(group == 0)
    def _():
        fill_bias(here, parts, docs_ref[...], bias)

    keys = [part[pl.ds(0, TOK), :] for part in parts]
    values = [window_part(value_own, value_pairs, REACH - k)[...] for k in range(BLOCKS)]
    for k in range(BLOCKS):
        keys_t[:, block(k)] = keys[k].astype(F32).T.astype(BF)
        values_t[:, block(k)] = values[k].astype(F32).T.astype(BF)
    for pair in range(PAIRS):
        q2 = pair_rows(q_ref, pair)
        g2 = pair_rows(g_ref, pair)
        lse2 = (
            jnp.concatenate(
                [lse_ref[0, 2 * pair + n : 2 * pair + n + 1, :] for n in range(2)], axis=1
            )
            * LOG2E
        )
        for k in range(BLOCKS):
            b = bias[block(k), :]
            t = dot(keys[k], q2, NT) * (INV_ROOT * LOG2E) + jnp.concatenate(
                [b, b], axis=1
            )
            w = jnp.exp2(t - lse2)
            weights32[block(k), :] = w
            weights[block(k), :] = w.astype(BF)
        out_t = dot(values_t[...], weights[...]).astype(BF).astype(F32)
        g2_t = jnp.concatenate(
            [g2[n * TOK : (n + 1) * TOK].astype(F32).T for n in range(2)], axis=1
        )
        delta = jnp.sum(out_t * g2_t, axis=0, keepdims=True)
        for k in range(BLOCKS):
            d_prob = dot(values[k], g2, NT)
            d_scores[block(k), pl.ds(pair * 2 * TOK, 2 * TOK)] = (
                weights32[block(k), :] * (d_prob - delta)
            ).astype(BF)
        dq_t = dot(keys_t[...], d_scores[:, pl.ds(pair * 2 * TOK, 2 * TOK)]) * INV_ROOT
        for n in range(2):
            head = slice((2 * pair + n) * HEAD, (2 * pair + n + 1) * HEAD)
            out_ref[:, head] = out_t[:, n * TOK : (n + 1) * TOK].T.astype(BF)
            dq_ref[:, head] = dq_t[:, n * TOK : (n + 1) * TOK].T.astype(BF)
    rows = jnp.concatenate([pair_rows(q_ref, pair) for pair in range(PAIRS)], axis=0)
    put_partials(
        dk_refs, lambda k: (dot(d_scores[block(k), :], rows) * INV_ROOT).astype(BF)
    )


def smem():
    return pl.BlockSpec(memory_space=pltpu.SMEM)


def anywhere():
    return pl.BlockSpec(memory_space=pl.ANY)


def partial_outs():
    counts = (3, 2, 2, 2)
    shapes = [jax.ShapeDtypeStruct((n, TOK, KV), BF) for n in counts]
    return shapes, [pl.BlockSpec((n, TOK, HEAD), lambda g: (0, 0, g)) for n in counts]


def window_specs(rows):
    own = pl.BlockSpec((rows, HEAD), lambda g: (0, g))
    pair = pl.BlockSpec((2, rows, HEAD), lambda g: (0, 0, g))
    return [own] * 3 + [pair] * 3


def run_scores(here, docs_own, owners, queries, grads, keys, after):
    shapes, specs = partial_outs()
    wide = pl.BlockSpec((TOK, PER_GROUP * HEAD), lambda g: (0, g))
    line = pl.BlockSpec((1, TOK), lambda g: (0, 0))
    return pl.pallas_call(
        scores_kernel,
        grid=(GROUPS,),
        in_specs=[smem(), line, line, wide, wide] + window_specs(PACK) + [anywhere()],
        out_specs=[
            pl.BlockSpec((1, PER_GROUP, TOK), lambda g: (g, 0, 0)),
            pl.BlockSpec((16, 1, CAP * HQ), lambda g: (0, 0, 0)),
        ]
        + specs,
        out_shape=[
            jax.ShapeDtypeStruct((GROUPS, PER_GROUP, TOK), F32),
            jax.ShapeDtypeStruct((16, 1, CAP * HQ), F32),
        ]
        + shapes,
        scratch_shapes=[
            pltpu.VMEM((KEYS, TOK), F32),
            pltpu.VMEM((KEYS, 2 * TOK), F32),
            pltpu.VMEM((KEYS, PER_GROUP * TOK), BF),
            pltpu.VMEM((HQ, TOK), F32),
        ],
        compiler_params=pltpu.CompilerParams(
            vmem_limit_bytes=VMEM, dimension_semantics=("arbitrary",)
        ),
        cost_estimate=pl.CostEstimate(
            flops=32 << 30, bytes_accessed=6 << 20, transcendentals=2 * HQ * TOK * KEYS
        ),
        name="scores",
    )(here, docs_own, owners, queries, grads, *keys, after)


def run_grads(here, docs_own, queries, grads, lse, keys, values):
    shapes, specs = partial_outs()
    wide = pl.BlockSpec((TOK, PER_GROUP * HEAD), lambda g: (0, g))
    return pl.pallas_call(
        grads_kernel,
        grid=(GROUPS,),
        in_specs=[
            smem(),
            pl.BlockSpec((1, TOK), lambda g: (0, 0)),
            wide,
            wide,
            pl.BlockSpec((1, PER_GROUP, TOK), lambda g: (g, 0, 0)),
        ]
        + window_specs(PACK)
        + window_specs(TOK),
        out_specs=[wide, wide] + specs,
        out_shape=[jax.ShapeDtypeStruct((TOK, HQ * HEAD), BF)] * 2 + shapes,
        scratch_shapes=[
            pltpu.VMEM((KEYS, TOK), F32),
            pltpu.VMEM((HEAD, KEYS), BF),
            pltpu.VMEM((HEAD, KEYS), BF),
            pltpu.VMEM((KEYS, 2 * TOK), F32),
            pltpu.VMEM((KEYS, 2 * TOK), BF),
            pltpu.VMEM((KEYS, PER_GROUP * TOK), BF),
        ],
        compiler_params=pltpu.CompilerParams(
            vmem_limit_bytes=VMEM, dimension_semantics=("arbitrary",)
        ),
        cost_estimate=pl.CostEstimate(
            flops=64 << 30, bytes_accessed=8 << 20, transcendentals=HQ * TOK * KEYS
        ),
        name="grads",
    )(here, docs_own, queries, grads, lse, *keys, *values)


def along_z(x, step):
    return lax.ppermute(x, "ctx", [(i, i // 4 * 4 + (i + step) % 4) for i in range(16)])


def along_x(x, step):
    return lax.ppermute(x, "ctx", [(i, (i + 4 * step) % 16) for i in range(16)])


def along_y(x, step):
    return lax.ppermute(x, "dp", [(i, (i + 2 * step) % 8) for i in range(8)])


def other_core(x):
    return lax.ppermute(x, "dp", [(i, i ^ 1) for i in range(8)])


def for_peers(own, z):
    blocks = [own, along_x(own, 1), along_x(own, 2)]
    own, row_1, row_2 = blocks
    pairs = []
    for e in (1, 2, 3):
        wrapped = z + e > 3
        pairs.append(jnp.stack([jnp.where(wrapped, row_1, own), jnp.where(wrapped, row_2, row_1)]))
    return blocks, pairs


def to_peers(pairs):
    return [along_z(pair, e) for e, pair in zip((1, 2, 3), pairs)]


def across(x, axis_step):
    return lax.ppermute(x, "ctx", [(i, i ^ axis_step) for i in range(16)])


def swap_sum(x, axis_step, after=()):
    (total,) = small_call(
        swap_sum_kernel,
        in_vmem(2) + [anywhere()] * len(after),
        [(x.shape, BF)],
        "swap_sum",
        1,
    )(x, across(x, axis_step), *after)
    return total


def swap_sum_kernel(own, got, *refs):
    refs[-1][...] = (own[...].astype(F32) + got[...].astype(F32)).astype(BF)


def in_vmem(count):
    return [pl.BlockSpec(memory_space=pltpu.VMEM)] * count


def small_call(kernel, specs, shapes, name, us, scratch=(), grid=()):
    return pl.pallas_call(
        kernel,
        grid=grid,
        in_specs=specs,
        out_specs=in_vmem(len(shapes)),
        out_shape=[jax.ShapeDtypeStruct(shape, dtype) for shape, dtype in shapes],
        scratch_shapes=list(scratch),
        compiler_params=pltpu.CompilerParams(vmem_limit_bytes=SMALL_VMEM),
        cost_estimate=pl.CostEstimate(
            flops=us << 30, bytes_accessed=us << 21, transcendentals=0
        ),
        name=name,
    )


def values_kernel(product, low_rank, up, _after, out):
    out[...] = (product[...] + ADAPTER_SCALE * dot(low_rank[...], up[...])).astype(BF)


def gate_kernel(*refs):
    pass


def gate(arrays, after):
    return pl.pallas_call(
        gate_kernel,
        in_specs=[anywhere()] * (len(arrays) + 1),
        out_specs=[anywhere()] * len(arrays),
        out_shape=[jax.ShapeDtypeStruct(array.shape, array.dtype) for array in arrays],
        input_output_aliases={n: n for n in range(len(arrays))},
        name="gate",
    )(*arrays, after)


def sum_terms(terms):
    total = terms[0][...].astype(F32)
    for term in terms[1:]:
        total = total + term[...].astype(F32)
    return total.astype(BF)


def key_grad_kernel(*refs):
    refs[-1][...] = sum_terms(refs[:-1])


def row_sums_kernel(z_ref, own, *refs):
    *got, _after, here_out, near_out, far_out = refs
    here_row, row_1, row_2 = (own[n].astype(F32) for n in range(3))
    for n, pair in enumerate(got):
        before = z_ref[0] + 1 + n > 3
        near, far = pair[0].astype(F32), pair[1].astype(F32)
        here_row = here_row + jnp.where(before, 0.0, near)
        row_1 = row_1 + jnp.where(before, near, far)
        row_2 = row_2 + jnp.where(before, far, 0.0)
    here_out[...] = here_row
    near_out[...] = row_1.astype(BF)
    far_out[...] = row_2.astype(BF)


def sum_kernel(*refs):
    refs[-1][...] = sum_terms(refs[:4])


def adapter_kernel(core_ref, *refs):
    up, low_rank, rows, grad_out, middle_out, keep_out, send_out = refs[3:]
    grad = sum_terms(refs[:3])
    grad_out[...] = grad
    middle = (ADAPTER_SCALE * dot(grad, up[...], NT)).astype(BF)
    middle_out[...] = middle
    middle_t = middle.astype(F32).T.astype(BF)
    low_rank_t = low_rank[...].astype(F32).T.astype(BF)
    half = keep_out.shape[0]
    model = rows.shape[1]
    first = core_ref[0] == 0

    def split(part, columns):
        low, high = part[:half].astype(BF), part[half:].astype(BF)
        keep_out[:, columns] = jnp.where(first, low, high)
        send_out[:, columns] = jnp.where(first, high, low)

    step = 1024
    for n in range(model // step):
        columns = slice(n * step, (n + 1) * step)
        split(dot(middle_t, rows[:, columns]), columns)
    split(ADAPTER_SCALE * dot(low_rank_t, grad), slice(model, model + KV))


def quarters_kernel(y_ref, keep, got, mine_out, *send_outs):
    part = mine_out.shape[1]
    for e, out in enumerate((mine_out,) + send_outs):
        first = lax.rem(y_ref[0] + e, 4) * part
        columns = pl.ds(pl.multiple_of(first, HEAD), part)
        out[...] = (keep[:, columns].astype(F32) + got[:, columns].astype(F32)).astype(BF)


def assemble_kernel(y_ref, *refs):
    *parts, _d_key, _slots, out = refs
    width = parts[0].shape[1]
    for e, part in enumerate(parts):
        first = lax.rem(y_ref[0] + 4 - e, 4) * width
        out[:, pl.ds(pl.multiple_of(first, HEAD), width)] = part[...]


def totals_kernel(core_ref, mine, other, down_out, up_out):
    half = mine.shape[0]
    model = down_out.shape[1]
    first = core_ref[0] == 0
    step = 512

    def whole(columns):
        a, b = mine[:, columns].astype(F32), other[:, columns].astype(F32)
        return jnp.concatenate([jnp.where(first, a, b), jnp.where(first, b, a)], axis=0)

    for n in range(model // step):
        columns = slice(n * step, (n + 1) * step)
        down_out[:, columns] = whole(columns)
    up_out[...] = whole(slice(model, model + KV))


def slots_kernel(got, out, rows):
    for slot in range(CAP):
        rows[pl.ds(slot, got.shape[0], stride=CAP), 0:HQ] = got[:, 0, slot * HQ : (slot + 1) * HQ]
    out[...] = rows[...].T[:HQ]


def sum_home(parts, z, after):
    got = [along_z(part, -distance) for distance, part in zip((3, 2, 1), parts[1:])]
    here_row, near, far = small_call(
        row_sums_kernel,
        [smem()] + in_vmem(4) + [anywhere()],
        [((TOK, KV), F32), ((TOK, KV), BF), ((TOK, KV), BF)],
        "row_sums",
        1,
    )(z, parts[0], *got[::-1], after)
    return here_row, along_x(near, -1), along_x(far, -2)


def local(
    normed,
    queries,
    rotated_keys,
    value_weight,
    adapter_down,
    adapter_up,
    attention_cotangent,
    document_index,
    owner_routing,
):
    ctx = lax.axis_index("ctx")
    dp = lax.axis_index("dp")
    y, core = dp // 2, dp % 2
    rows = normed[0]
    low_rank = dot(rows, adapter_down).astype(BF)
    doc_rows = jnp.broadcast_to(
        jnp.tile(document_index.astype(BF), (1, KV // TOK)), (DOC_ROWS, KV)
    )
    z = ctx % 4
    key_own, key_pairs = for_peers(jnp.concatenate([rotated_keys[0], doc_rows], axis=0), z)
    (values,) = small_call(
        values_kernel, in_vmem(3) + [anywhere()], [((TOK, KV), BF)], "values", 1
    )(dot(rows, value_weight), low_rank, adapter_up, key_own[1])
    value_own, value_pairs = for_peers(values, z)
    key_parts = key_own + to_peers(key_pairs)
    value_parts = value_own + to_peers(value_pairs)
    here, z, y, core = (n.reshape(1) for n in (ctx, z, y, core))
    lse, own_lse, *dv_parts = run_scores(
        here,
        document_index,
        owner_routing.reshape(1, TOK),
        queries[0],
        attention_cotangent[0],
        key_parts,
        value_pairs[0],
    )
    out, dq, *dk_parts = run_grads(
        here, document_index, queries[0], attention_cotangent[0], lse, key_parts, value_parts
    )
    peers = lax.axis_size("ctx")
    got_lse = lax.all_to_all(own_lse, "ctx", split_axis=0, concat_axis=0, tiled=True)
    (lse_rows,) = small_call(
        slots_kernel,
        in_vmem(1),
        [((HQ, peers * CAP), F32)],
        "slots",
        1,
        [pltpu.VMEM((peers * CAP, TOK), F32)],
    )(got_lse)

    dv_terms = sum_home(dv_parts, z, dq)

    rank, model = adapter_up.shape[0], rows.shape[1]
    half, width = rank // 2, model + KV
    part = width // 4
    value_grad, middle, keep, send = small_call(
        adapter_kernel,
        [smem()] + in_vmem(6),
        [((TOK, KV), BF), ((TOK, rank), BF), ((half, width), BF), ((half, width), BF)],
        "adapter",
        3,
    )(core, *dv_terms, adapter_up, low_rank, rows)
    mine, *sends = small_call(
        quarters_kernel, [smem()] + in_vmem(2), [((half, part), BF)] * 4, "quarters", 1
    )(y, keep, other_core(send))
    normed_input_gradient = (
        dot(value_grad, value_weight, NT) + dot(middle, adapter_down, NT)
    ).astype(BF)
    (mine,) = small_call(
        sum_kernel, in_vmem(4) + [anywhere()], [((half, part), BF)], "y_sum", 1
    )(mine, *[along_y(send, e) for e, send in zip((1, 2, 3), sends)], normed_input_gradient)
    dk_parts[1:] = gate(dk_parts[1:], mine)
    dk_terms = sum_home(dk_parts, z, here)
    (d_key,) = small_call(key_grad_kernel, in_vmem(3), [((TOK, KV), BF)], "key_grad", 1)(*dk_terms)
    for axis_step in (4, 8, 1, 2):
        mine = swap_sum(mine, axis_step)
    (whole,) = small_call(
        assemble_kernel,
        [smem()] + in_vmem(4) + [anywhere()] * 2,
        [((half, width), BF)],
        "assemble",
        1,
    )(y, mine, *[along_y(mine, e) for e in (1, 2, 3)], d_key, lse_rows)
    total_down, total_up = small_call(
        totals_kernel, [smem()] + in_vmem(2), [((rank, model), F32), ((rank, KV), F32)], "totals", 2
    )(core, whole, other_core(whole))

    return (
        out[None],
        dq[None],
        d_key[None],
        normed_input_gradient[None],
        total_down.T,
        total_up,
        lse_rows.T[None],
    )


def solution(mesh):
    tokens = P("dp", "ctx", None)
    return jax.shard_map(
        local,
        mesh=mesh,
        in_specs=(tokens, tokens, tokens, P(), P(), P(), tokens, P("dp", "ctx"), tokens),
        out_specs=(tokens, tokens, tokens, tokens, P(), P(), tokens),
        check_vma=False,
    )
```

```python
import functools
import math

import jax
import jax.numpy as jnp
from jax import lax
from jax.experimental import pallas as pl
from jax.experimental.pallas import tpu as pltpu
from jax.sharding import PartitionSpec as P

HEAD = 128
HQ = 32
GROUPS = 4
PER_GROUP = HQ // GROUPS
PAIRS = PER_GROUP // 2
CAP = 12
TOK = 128
REACH = 8
BLOCKS = REACH + 1
KEYS = BLOCKS * TOK
DOC_ROWS = 16
PACK = TOK + DOC_ROWS
KV = GROUPS * HEAD
ADAPTER_SCALE = 0.5
INV_ROOT = 1.0 / math.sqrt(HEAD)
LOG2E = 1.4426950408889634
LN2 = 0.6931471805599453
MASKED = -1e30
VMEM = 56 << 20
SMALL_VMEM = 20 << 20
BF = jnp.bfloat16
F32 = jnp.float32
NT = (((1,), (1,)), ((), ()))
NN = (((1,), (0,)), ((), ()))


def dot(a, b, dims=NN):
    return lax.dot_general(a, b, dims, preferred_element_type=F32)


def window_part(own, pairs, distance):
    if distance % 4 == 0:
        return own[distance // 4]
    return pairs[distance % 4 - 1].at[distance // 4]


def put_partials(outs, value_of):
    for distance in range(BLOCKS):
        outs[-distance % 4][distance // 4] = value_of(REACH - distance)


def fill_bias(here, parts, docs_own, bias):
    own = docs_own.astype(F32)
    real = [jnp.where(here - REACH + k >= 0, 1.0, 0.0) for k in range(BLOCKS)]
    docs = [parts[k][pl.ds(TOK, DOC_ROWS), :].astype(F32) for k in range(BLOCKS)]
    missing = jnp.maximum(REACH - here, 0) * TOK
    start = jnp.zeros((1, TOK), F32)
    for number in (1, 2, 3):
        lower = jnp.zeros((DOC_ROWS, TOK), F32)
        for k in range(BLOCKS):
            lower = lower + jnp.where(docs[k] < number, real[k], 0.0)
        start = jnp.where(own == number, jnp.sum(lower) / DOC_ROWS, start)
    first = start.astype(jnp.int32) + missing
    lane = lax.broadcasted_iota(jnp.int32, (TOK, TOK), 1)
    row = lax.broadcasted_iota(jnp.int32, (TOK, TOK), 0)
    for k in range(BLOCKS):
        spot = row + k * TOK
        seen = (spot >= first) & (spot <= REACH * TOK + lane)
        bias[pl.ds(k * TOK, TOK), :] = jnp.where(seen, 0.0, MASKED)


def pair_rows(ref, pair):
    return jnp.concatenate(
        [ref[:, (2 * pair + n) * HEAD : (2 * pair + n + 1) * HEAD] for n in range(2)], axis=0
    )


def block(k):
    return pl.ds(k * TOK, TOK)


def fold(x, op):
    return op(x.reshape(TOK // 8, 8, 2 * TOK), axis=0)


def scores_kernel(here_ref, docs_ref, owners_ref, q_ref, g_ref, *rest):
    key_own, key_pairs = rest[:3], rest[3:6]
    lse_ref, slots_ref, *dv_refs = rest[7:13]
    bias, scores, weights, lse_all = rest[13:]
    parts = [window_part(key_own, key_pairs, REACH - k) for k in range(BLOCKS)]
    group = pl.program_id(0)
    here = here_ref[0]

    @pl.when(group == 0)
    def _():
        fill_bias(here, parts, docs_ref[...], bias)

    keys = [part[pl.ds(0, TOK), :] for part in parts]
    rows = []
    for pair in range(PAIRS):
        q2 = pair_rows(q_ref, pair)
        peak = jnp.full((8, 2 * TOK), MASKED, F32)
        for k in range(BLOCKS):
            b = bias[block(k), :]
            t = dot(keys[k], q2, NT) * (INV_ROOT * LOG2E) + jnp.concatenate(
                [b, b], axis=1
            )
            scores[block(k), :] = t
            peak = jnp.maximum(peak, fold(t, jnp.max))
        peak = jnp.max(peak, axis=0, keepdims=True)
        total = jnp.zeros((8, 2 * TOK), F32)
        for k in range(BLOCKS):
            p = jnp.exp2(scores[block(k), :] - peak)
            total = total + fold(p, jnp.sum)
            weights[block(k), pl.ds(pair * 2 * TOK, 2 * TOK)] = p.astype(BF)
        total = jnp.sum(total, axis=0, keepdims=True)
        lse2 = peak + jnp.log2(total)
        share = 1.0 / total
        for n in range(2):
            lse = lse2[:, n * TOK : (n + 1) * TOK] * LN2
            lse_ref[0, 2 * pair + n : 2 * pair + n + 1, :] = lse
            lse_all[pl.ds(group * PER_GROUP + 2 * pair + n, 1), :] = lse
            column = jnp.broadcast_to(share[:, n * TOK : (n + 1) * TOK], (TOK, TOK)).T
            head = slice((2 * pair + n) * HEAD, (2 * pair + n + 1) * HEAD)
            rows.append((g_ref[:, head].astype(F32) * column).astype(BF))
    rows = jnp.concatenate(rows, axis=0)
    put_partials(dv_refs, lambda k: dot(weights[block(k), :], rows).astype(BF))

    @pl.when(group == GROUPS - 1)
    def _():
        put_slots(owners_ref[...], lse_all[...], slots_ref)


def put_slots(owners, lse, slots_ref):
    peers = slots_ref.shape[0]
    named = lax.broadcasted_iota(jnp.int32, (peers, TOK), 0) == owners
    onehot = jnp.where(named, 1.0, 0.0)
    before = lax.broadcasted_iota(jnp.int32, (TOK, TOK), 0) < lax.broadcasted_iota(
        jnp.int32, (TOK, TOK), 1
    )
    earlier = dot(onehot.astype(BF), jnp.where(before, 1.0, 0.0).astype(BF))
    for slot in range(CAP):
        place = jnp.where(named & (earlier == slot), 1.0, 0.0)
        slots_ref[:, 0, slot * HQ : (slot + 1) * HQ] = lax.dot_general(
            place, lse, NT, precision=lax.Precision.HIGHEST, preferred_element_type=F32
        )


def grads_kernel(here_ref, docs_ref, q_ref, g_ref, lse_ref, *rest):
    key_own, key_pairs, value_own, value_pairs = rest[:3], rest[3:6], rest[6:9], rest[9:12]
    out_ref, dq_ref, *dk_refs = rest[-12:-6]
    bias, keys_t, values_t, weights32, weights, d_scores = rest[-6:]
    parts = [window_part(key_own, key_pairs, REACH - k) for k in range(BLOCKS)]
    group = pl.program_id(0)
    here = here_ref[0]

    @pl.when(group == 0)
    def _():
        fill_bias(here, parts, docs_ref[...], bias)

    keys = [part[pl.ds(0, TOK), :] for part in parts]
    values = [window_part(value_own, value_pairs, REACH - k)[...] for k in range(BLOCKS)]
    for k in range(BLOCKS):
        keys_t[:, block(k)] = keys[k].astype(F32).T.astype(BF)
        values_t[:, block(k)] = values[k].astype(F32).T.astype(BF)
    for pair in range(PAIRS):
        q2 = pair_rows(q_ref, pair)
        g2 = pair_rows(g_ref, pair)
        lse2 = (
            jnp.concatenate(
                [lse_ref[0, 2 * pair + n : 2 * pair + n + 1, :] for n in range(2)], axis=1
            )
            * LOG2E
        )
        for k in range(BLOCKS):
            b = bias[block(k), :]
            t = dot(keys[k], q2, NT) * (INV_ROOT * LOG2E) + jnp.concatenate(
                [b, b], axis=1
            )
            w = jnp.exp2(t - lse2)
            weights32[block(k), :] = w
            weights[block(k), :] = w.astype(BF)
        out_t = dot(values_t[...], weights[...]).astype(BF).astype(F32)
        g2_t = jnp.concatenate(
            [g2[n * TOK : (n + 1) * TOK].astype(F32).T for n in range(2)], axis=1
        )
        delta = jnp.sum(out_t * g2_t, axis=0, keepdims=True)
        for k in range(BLOCKS):
            d_prob = dot(values[k], g2, NT)
            d_scores[block(k), pl.ds(pair * 2 * TOK, 2 * TOK)] = (
                weights32[block(k), :] * (d_prob - delta)
            ).astype(BF)
        dq_t = dot(keys_t[...], d_scores[:, pl.ds(pair * 2 * TOK, 2 * TOK)]) * INV_ROOT
        for n in range(2):
            head = slice((2 * pair + n) * HEAD, (2 * pair + n + 1) * HEAD)
            out_ref[:, head] = out_t[:, n * TOK : (n + 1) * TOK].T.astype(BF)
            dq_ref[:, head] = dq_t[:, n * TOK : (n + 1) * TOK].T.astype(BF)
    rows = jnp.concatenate([pair_rows(q_ref, pair) for pair in range(PAIRS)], axis=0)
    put_partials(
        dk_refs, lambda k: (dot(d_scores[block(k), :], rows) * INV_ROOT).astype(BF)
    )


def smem():
    return pl.BlockSpec(memory_space=pltpu.SMEM)


def anywhere():
    return pl.BlockSpec(memory_space=pl.ANY)


def partial_outs(first=0):
    counts = (3, 2, 2, 2)
    shapes = [jax.ShapeDtypeStruct((n, TOK, KV), BF) for n in counts]
    return shapes, [pl.BlockSpec((n, TOK, HEAD), lambda g: (0, 0, g + first)) for n in counts]


def window_specs(rows, first=0):
    own = pl.BlockSpec((rows, HEAD), lambda g: (0, g + first))
    pair = pl.BlockSpec((2, rows, HEAD), lambda g: (0, 0, g + first))
    return [own] * 3 + [pair] * 3


def run_scores(here, docs_own, owners, queries, grads, keys, after):
    shapes, specs = partial_outs()
    wide = pl.BlockSpec((TOK, PER_GROUP * HEAD), lambda g: (0, g))
    line = pl.BlockSpec((1, TOK), lambda g: (0, 0))
    return pl.pallas_call(
        scores_kernel,
        grid=(GROUPS,),
        in_specs=[smem(), line, line, wide, wide] + window_specs(PACK) + [anywhere()],
        out_specs=[
            pl.BlockSpec((1, PER_GROUP, TOK), lambda g: (g, 0, 0)),
            pl.BlockSpec((16, 1, CAP * HQ), lambda g: (0, 0, 0)),
        ]
        + specs,
        out_shape=[
            jax.ShapeDtypeStruct((GROUPS, PER_GROUP, TOK), F32),
            jax.ShapeDtypeStruct((16, 1, CAP * HQ), F32),
        ]
        + shapes,
        scratch_shapes=[
            pltpu.VMEM((KEYS, TOK), F32),
            pltpu.VMEM((KEYS, 2 * TOK), F32),
            pltpu.VMEM((KEYS, PER_GROUP * TOK), BF),
            pltpu.VMEM((HQ, TOK), F32),
        ],
        compiler_params=pltpu.CompilerParams(
            vmem_limit_bytes=VMEM, dimension_semantics=("arbitrary",)
        ),
        cost_estimate=pl.CostEstimate(
            flops=32 << 30, bytes_accessed=6 << 20, transcendentals=2 * HQ * TOK * KEYS
        ),
        name="scores",
    )(here, docs_own, owners, queries, grads, *keys, after)


def run_grads(here, docs_own, queries, grads, lse, keys, values, first, count, begun=()):
    shapes, specs = partial_outs(first)
    wide = pl.BlockSpec((TOK, PER_GROUP * HEAD), lambda g: (0, g + first))
    return pl.pallas_call(
        grads_kernel,
        grid=(count,),
        in_specs=[
            smem(),
            pl.BlockSpec((1, TOK), lambda g: (0, 0)),
            wide,
            wide,
            pl.BlockSpec((1, PER_GROUP, TOK), lambda g: (g + first, 0, 0)),
        ]
        + window_specs(PACK, first)
        + window_specs(TOK, first)
        + [anywhere()] * len(begun),
        out_specs=[wide, wide] + specs,
        out_shape=[jax.ShapeDtypeStruct((TOK, HQ * HEAD), BF)] * 2 + shapes,
        scratch_shapes=[
            pltpu.VMEM((KEYS, TOK), F32),
            pltpu.VMEM((HEAD, KEYS), BF),
            pltpu.VMEM((HEAD, KEYS), BF),
            pltpu.VMEM((KEYS, 2 * TOK), F32),
            pltpu.VMEM((KEYS, 2 * TOK), BF),
            pltpu.VMEM((KEYS, PER_GROUP * TOK), BF),
        ],
        input_output_aliases={17 + n: n for n in range(len(begun))},
        compiler_params=pltpu.CompilerParams(
            vmem_limit_bytes=VMEM, dimension_semantics=("arbitrary",)
        ),
        cost_estimate=pl.CostEstimate(
            flops=32 << 30, bytes_accessed=8 << 20, transcendentals=HQ * TOK * KEYS
        ),
        name="grads_%d" % first,
    )(here, docs_own, queries, grads, lse, *keys, *values, *begun)


def along_z(x, step):
    return lax.ppermute(x, "ctx", [(i, i // 4 * 4 + (i + step) % 4) for i in range(16)])


def along_x(x, step):
    return lax.ppermute(x, "ctx", [(i, (i + 4 * step) % 16) for i in range(16)])


def along_y(x, step):
    return lax.ppermute(x, "dp", [(i, (i + 2 * step) % 8) for i in range(8)])


def other_core(x):
    return lax.ppermute(x, "dp", [(i, i ^ 1) for i in range(8)])


def pick_kernel(z_ref, own, row_1, row_2, *outs):
    for e, out in zip((1, 2, 3), outs):
        wrapped = z_ref[0] + e > 3
        out[0] = jnp.where(wrapped, row_1[...], own[...])
        out[1] = jnp.where(wrapped, row_2[...], row_1[...])


def for_peers(own, z):
    blocks = [own, along_x(own, 1), along_x(own, 2)]
    pairs = small_call(
        pick_kernel, [smem()] + in_vmem(3), [((2, *own.shape), BF)] * 3, "pick", 1
    )(z, *blocks)
    return blocks, list(pairs)


def to_peers(pairs):
    return [along_z(pair, e) for e, pair in zip((1, 2, 3), pairs)]


def across(x, axis_step):
    return lax.ppermute(x, "ctx", [(i, i ^ axis_step) for i in range(16)])


def swap_sum(x, axis_step, after=()):
    (total,) = small_call(
        swap_sum_kernel,
        in_vmem(2) + [anywhere()] * len(after),
        [(x.shape, BF)],
        "swap_sum",
        1,
    )(x, across(x, axis_step), *after)
    return total


def swap_sum_kernel(own, got, *refs):
    refs[-1][...] = (own[...].astype(F32) + got[...].astype(F32)).astype(BF)


def in_vmem(count):
    return [pl.BlockSpec(memory_space=pltpu.VMEM)] * count


def small_call(kernel, specs, shapes, name, us, scratch=(), grid=()):
    return pl.pallas_call(
        kernel,
        grid=grid,
        in_specs=specs,
        out_specs=in_vmem(len(shapes)),
        out_shape=[jax.ShapeDtypeStruct(shape, dtype) for shape, dtype in shapes],
        scratch_shapes=list(scratch),
        compiler_params=pltpu.CompilerParams(vmem_limit_bytes=SMALL_VMEM),
        cost_estimate=pl.CostEstimate(
            flops=us << 30, bytes_accessed=us << 21, transcendentals=0
        ),
        name=name,
    )


def pack_kernel(keys, docs, out):
    out[0:TOK, :] = keys[...]
    rows = jnp.broadcast_to(docs[...].astype(F32), (DOC_ROWS, TOK)).astype(BF)
    for group in range(GROUPS):
        out[TOK:PACK, group * HEAD : (group + 1) * HEAD] = rows


def gate_kernel(*refs):
    pass


def gate(arrays, after):
    return pl.pallas_call(
        gate_kernel,
        in_specs=[anywhere()] * (len(arrays) + 1),
        out_specs=[anywhere()] * len(arrays),
        out_shape=[jax.ShapeDtypeStruct(array.shape, array.dtype) for array in arrays],
        input_output_aliases={n: n for n in range(len(arrays))},
        name="gate",
    )(*arrays, after)


def sum_terms(terms):
    total = terms[0][...].astype(F32)
    for term in terms[1:]:
        total = total + term[...].astype(F32)
    return total.astype(BF)


def key_grad_kernel(*refs):
    refs[-1][...] = sum_terms(refs[:-1])


def row_sums_kernel(z_ref, own, *refs):
    *got, _after, here_out, near_out, far_out = refs
    here_row, row_1, row_2 = (own[n].astype(F32) for n in range(3))
    for n, pair in enumerate(got):
        before = z_ref[0] + 1 + n > 3
        near, far = pair[0].astype(F32), pair[1].astype(F32)
        here_row = here_row + jnp.where(before, 0.0, near)
        row_1 = row_1 + jnp.where(before, near, far)
        row_2 = row_2 + jnp.where(before, far, 0.0)
    here_out[...] = here_row
    near_out[...] = row_1.astype(BF)
    far_out[...] = row_2.astype(BF)


def sum_kernel(*refs):
    refs[-1][...] = sum_terms(refs[:4])


def adapter_kernel(core_ref, *refs):
    up, low_rank, rows, _after, grad_out, middle_out, keep_out, send_out = refs[3:]
    grad = sum_terms(refs[:3])
    grad_out[...] = grad
    middle = (ADAPTER_SCALE * dot(grad, up[...], NT)).astype(BF)
    middle_out[...] = middle
    middle_t = middle.astype(F32).T.astype(BF)
    low_rank_t = low_rank[...].astype(F32).T.astype(BF)
    half = keep_out.shape[0]
    model = rows.shape[1]
    first = core_ref[0] == 0

    def split(part, columns):
        low, high = part[:half].astype(BF), part[half:].astype(BF)
        keep_out[:, columns] = jnp.where(first, low, high)
        send_out[:, columns] = jnp.where(first, high, low)

    step = 1024
    for n in range(model // step):
        columns = slice(n * step, (n + 1) * step)
        split(dot(middle_t, rows[:, columns]), columns)
    split(ADAPTER_SCALE * dot(low_rank_t, grad), slice(model, model + KV))


def quarters_kernel(y_ref, keep, got, mine_out, *send_outs):
    part = mine_out.shape[1]
    for e, out in enumerate((mine_out,) + send_outs):
        first = lax.rem(y_ref[0] + e, 4) * part
        columns = pl.ds(pl.multiple_of(first, HEAD), part)
        out[...] = (keep[:, columns].astype(F32) + got[:, columns].astype(F32)).astype(BF)


def assemble_kernel(y_ref, *refs):
    *parts, _d_key, _slots, out = refs
    width = parts[0].shape[1]
    for e, part in enumerate(parts):
        first = lax.rem(y_ref[0] + 4 - e, 4) * width
        out[:, pl.ds(pl.multiple_of(first, HEAD), width)] = part[...]


def totals_kernel(core_ref, mine, other, down_out, up_out):
    half = mine.shape[0]
    model = down_out.shape[1]
    first = core_ref[0] == 0
    step = 512

    def whole(columns):
        a, b = mine[:, columns].astype(F32), other[:, columns].astype(F32)
        return jnp.concatenate([jnp.where(first, a, b), jnp.where(first, b, a)], axis=0)

    for n in range(model // step):
        columns = slice(n * step, (n + 1) * step)
        down_out[:, columns] = whole(columns)
    up_out[...] = whole(slice(model, model + KV))


def slots_kernel(got, out, rows):
    for slot in range(CAP):
        rows[pl.ds(slot, got.shape[0], stride=CAP), 0:HQ] = got[:, 0, slot * HQ : (slot + 1) * HQ]
    out[...] = rows[...].T[:HQ]


def sum_home(parts, z, after):
    got = [along_z(part, -distance) for distance, part in zip((3, 2, 1), parts[1:])]
    here_row, near, far = small_call(
        row_sums_kernel,
        [smem()] + in_vmem(4) + [anywhere()],
        [((TOK, KV), F32), ((TOK, KV), BF), ((TOK, KV), BF)],
        "row_sums",
        1,
    )(z, parts[0], *got[::-1], after)
    return here_row, along_x(near, -1), along_x(far, -2)


def local(
    normed,
    queries,
    rotated_keys,
    value_weight,
    adapter_down,
    adapter_up,
    attention_cotangent,
    document_index,
    owner_routing,
):
    ctx = lax.axis_index("ctx")
    dp = lax.axis_index("dp")
    y, core = dp // 2, dp % 2
    rows = normed[0]
    low_rank = dot(rows, adapter_down).astype(BF)
    values = (dot(rows, value_weight) + ADAPTER_SCALE * dot(low_rank, adapter_up)).astype(BF)
    z = (ctx % 4).reshape(1)
    (packed,) = small_call(pack_kernel, in_vmem(2), [((PACK, KV), BF)], "pack", 1)(
        rotated_keys[0], document_index
    )
    key_own, key_pairs = for_peers(packed, z)
    key_parts = key_own + to_peers(key_pairs)
    (values,) = gate([values], key_own[1])
    value_own, value_pairs = for_peers(values, z)
    value_parts = value_own + to_peers(value_pairs)
    here, y, core = (n.reshape(1) for n in (ctx, y, core))
    lse, own_lse, *dv_parts = run_scores(
        here,
        document_index,
        owner_routing.reshape(1, TOK),
        queries[0],
        attention_cotangent[0],
        key_parts,
        value_pairs[0],
    )
    args = (here, document_index, queries[0], attention_cotangent[0], lse, key_parts, value_parts)
    half_done = run_grads(*args, 0, GROUPS // 2)
    out, dq, *dk_parts = run_grads(*args, GROUPS // 2, GROUPS - GROUPS // 2, half_done)

    peers = lax.axis_size("ctx")
    got_lse = lax.all_to_all(own_lse, "ctx", split_axis=0, concat_axis=0, tiled=True)
    (lse_rows,) = small_call(
        slots_kernel,
        in_vmem(1),
        [((HQ, peers * CAP), F32)],
        "slots",
        1,
        [pltpu.VMEM((peers * CAP, TOK), F32)],
    )(got_lse)

    dv_terms = sum_home(dv_parts, z, half_done[1])

    rank, model = adapter_up.shape[0], rows.shape[1]
    half, width = rank // 2, model + KV
    part = width // 4
    value_grad, middle, keep, send = small_call(
        adapter_kernel,
        [smem()] + in_vmem(6) + [anywhere()],
        [((TOK, KV), BF), ((TOK, rank), BF), ((half, width), BF), ((half, width), BF)],
        "adapter",
        3,
    )(core, *dv_terms, adapter_up, low_rank, rows, dq)
    mine, *sends = small_call(
        quarters_kernel, [smem()] + in_vmem(2), [((half, part), BF)] * 4, "quarters", 1
    )(y, keep, other_core(send))
    normed_input_gradient = (
        dot(value_grad, value_weight, NT) + dot(middle, adapter_down, NT)
    ).astype(BF)
    (mine,) = small_call(
        sum_kernel, in_vmem(4) + [anywhere()], [((half, part), BF)], "y_sum", 1
    )(mine, *[along_y(send, e) for e, send in zip((1, 2, 3), sends)], normed_input_gradient)
    dk_parts[1:] = gate(dk_parts[1:], mine)
    dk_terms = sum_home(dk_parts, z, here)
    (d_key,) = small_call(key_grad_kernel, in_vmem(3), [((TOK, KV), BF)], "key_grad", 1)(*dk_terms)
    for axis_step, after in ((4, ()), (8, ()), (1, (dk_terms[0],)), (2, ())):
        mine = swap_sum(mine, axis_step, after)
    (whole,) = small_call(
        assemble_kernel,
        [smem()] + in_vmem(4) + [anywhere()] * 2,
        [((half, width), BF)],
        "assemble",
        1,
    )(y, mine, *[along_y(mine, e) for e in (1, 2, 3)], d_key, lse_rows)
    total_down, total_up = small_call(
        totals_kernel, [smem()] + in_vmem(2), [((rank, model), F32), ((rank, KV), F32)], "totals", 2
    )(core, whole, other_core(whole))

    return (
        out[None],
        dq[None],
        d_key[None],
        normed_input_gradient[None],
        total_down.T,
        total_up,
        lse_rows.T[None],
    )


def solution(mesh):
    tokens = P("dp", "ctx", None)
    return jax.shard_map(
        local,
        mesh=mesh,
        in_specs=(tokens, tokens, tokens, P(), P(), P(), tokens, P("dp", "ctx"), tokens),
        out_specs=(tokens, tokens, tokens, tokens, P(), P(), tokens),
        check_vma=False,
    )
```

```python
import functools
import math

import jax
import jax.numpy as jnp
from jax import lax
from jax.experimental import pallas as pl
from jax.experimental.pallas import tpu as pltpu
from jax.sharding import PartitionSpec as P

HEAD = 128
HQ = 32
GROUPS = 4
PER_GROUP = HQ // GROUPS
PAIRS = PER_GROUP // 2
CAP = 12
TOK = 128
REACH = 8
BLOCKS = REACH + 1
KEYS = BLOCKS * TOK
DOC_ROWS = 16
PACK = TOK + DOC_ROWS
KV = GROUPS * HEAD
ADAPTER_SCALE = 0.5
INV_ROOT = 1.0 / math.sqrt(HEAD)
LOG2E = 1.4426950408889634
LN2 = 0.6931471805599453
MASKED = -1e30
VMEM = 56 << 20
SMALL_VMEM = 20 << 20
BF = jnp.bfloat16
F32 = jnp.float32
NT = (((1,), (1,)), ((), ()))
NN = (((1,), (0,)), ((), ()))


def dot(a, b, dims=NN):
    return lax.dot_general(a, b, dims, preferred_element_type=F32)


def window_part(own, pairs, distance):
    if distance % 4 == 0:
        return own[distance // 4]
    return pairs[distance % 4 - 1].at[distance // 4]


def put_partials(outs, value_of):
    for distance in range(BLOCKS):
        outs[-distance % 4][distance // 4] = value_of(REACH - distance)


def fill_bias(here, parts, docs_own, bias):
    own = docs_own.astype(F32)
    real = [jnp.where(here - REACH + k >= 0, 1.0, 0.0) for k in range(BLOCKS)]
    docs = [parts[k][pl.ds(TOK, DOC_ROWS), :].astype(F32) for k in range(BLOCKS)]
    missing = jnp.maximum(REACH - here, 0) * TOK
    start = jnp.zeros((1, TOK), F32)
    for number in (1, 2, 3):
        lower = jnp.zeros((DOC_ROWS, TOK), F32)
        for k in range(BLOCKS):
            lower = lower + jnp.where(docs[k] < number, real[k], 0.0)
        start = jnp.where(own == number, jnp.sum(lower) / DOC_ROWS, start)
    first = start.astype(jnp.int32) + missing
    lane = lax.broadcasted_iota(jnp.int32, (TOK, TOK), 1)
    row = lax.broadcasted_iota(jnp.int32, (TOK, TOK), 0)
    for k in range(BLOCKS):
        spot = row + k * TOK
        seen = (spot >= first) & (spot <= REACH * TOK + lane)
        bias[pl.ds(k * TOK, TOK), :] = jnp.where(seen, 0.0, MASKED)


def pair_rows(ref, pair):
    return jnp.concatenate(
        [ref[:, (2 * pair + n) * HEAD : (2 * pair + n + 1) * HEAD] for n in range(2)], axis=0
    )


def block(k):
    return pl.ds(k * TOK, TOK)


def fold(x, op):
    return op(x.reshape(TOK // 8, 8, 2 * TOK), axis=0)


def scores_kernel(here_ref, docs_ref, owners_ref, q_ref, g_ref, *rest):
    key_own, key_pairs = rest[:3], rest[3:6]
    lse_ref, slots_ref, *dv_refs = rest[7:13]
    bias, scores, weights, lse_all = rest[13:]
    parts = [window_part(key_own, key_pairs, REACH - k) for k in range(BLOCKS)]
    group = pl.program_id(0)
    here = here_ref[0]

    @pl.when(group == 0)
    def _():
        fill_bias(here, parts, docs_ref[...], bias)

    keys = [part[pl.ds(0, TOK), :] for part in parts]
    rows = []
    for pair in range(PAIRS):
        q2 = pair_rows(q_ref, pair)
        peak = jnp.full((8, 2 * TOK), MASKED, F32)
        for k in range(BLOCKS):
            b = bias[block(k), :]
            t = dot(keys[k], q2, NT) * (INV_ROOT * LOG2E) + jnp.concatenate(
                [b, b], axis=1
            )
            scores[block(k), :] = t
            peak = jnp.maximum(peak, fold(t, jnp.max))
        peak = jnp.max(peak, axis=0, keepdims=True)
        total = jnp.zeros((8, 2 * TOK), F32)
        for k in range(BLOCKS):
            p = jnp.exp2(scores[block(k), :] - peak)
            total = total + fold(p, jnp.sum)
            weights[block(k), pl.ds(pair * 2 * TOK, 2 * TOK)] = p.astype(BF)
        total = jnp.sum(total, axis=0, keepdims=True)
        lse2 = peak + jnp.log2(total)
        share = 1.0 / total
        for n in range(2):
            lse = lse2[:, n * TOK : (n + 1) * TOK] * LN2
            lse_ref[0, 2 * pair + n : 2 * pair + n + 1, :] = lse
            lse_all[pl.ds(group * PER_GROUP + 2 * pair + n, 1), :] = lse
            column = jnp.broadcast_to(share[:, n * TOK : (n + 1) * TOK], (TOK, TOK)).T
            head = slice((2 * pair + n) * HEAD, (2 * pair + n + 1) * HEAD)
            rows.append((g_ref[:, head].astype(F32) * column).astype(BF))
    rows = jnp.concatenate(rows, axis=0)
    put_partials(dv_refs, lambda k: dot(weights[block(k), :], rows).astype(BF))

    @pl.when(group == GROUPS - 1)
    def _():
        put_slots(owners_ref[...], lse_all[...], slots_ref)


def put_slots(owners, lse, slots_ref):
    peers = slots_ref.shape[0]
    named = lax.broadcasted_iota(jnp.int32, (peers, TOK), 0) == owners
    onehot = jnp.where(named, 1.0, 0.0)
    before = lax.broadcasted_iota(jnp.int32, (TOK, TOK), 0) < lax.broadcasted_iota(
        jnp.int32, (TOK, TOK), 1
    )
    earlier = dot(onehot.astype(BF), jnp.where(before, 1.0, 0.0).astype(BF))
    for slot in range(CAP):
        place = jnp.where(named & (earlier == slot), 1.0, 0.0)
        slots_ref[:, 0, slot * HQ : (slot + 1) * HQ] = lax.dot_general(
            place, lse, NT, precision=lax.Precision.HIGHEST, preferred_element_type=F32
        )


def grads_kernel(here_ref, docs_ref, q_ref, g_ref, lse_ref, *rest):
    key_own, key_pairs, value_own, value_pairs = rest[:3], rest[3:6], rest[6:9], rest[9:12]
    out_ref, dq_ref, *dk_refs = rest[-12:-6]
    bias, keys_t, values_t, weights32, weights, d_scores = rest[-6:]
    parts = [window_part(key_own, key_pairs, REACH - k) for k in range(BLOCKS)]
    group = pl.program_id(0)
    here = here_ref[0]

    @pl.when(group == 0)
    def _():
        fill_bias(here, parts, docs_ref[...], bias)

    keys = [part[pl.ds(0, TOK), :] for part in parts]
    values = [window_part(value_own, value_pairs, REACH - k)[...] for k in range(BLOCKS)]
    for k in range(BLOCKS):
        keys_t[:, block(k)] = keys[k].astype(F32).T.astype(BF)
        values_t[:, block(k)] = values[k].astype(F32).T.astype(BF)
    for pair in range(PAIRS):
        q2 = pair_rows(q_ref, pair)
        g2 = pair_rows(g_ref, pair)
        lse2 = (
            jnp.concatenate(
                [lse_ref[0, 2 * pair + n : 2 * pair + n + 1, :] for n in range(2)], axis=1
            )
            * LOG2E
        )
        for k in range(BLOCKS):
            b = bias[block(k), :]
            t = dot(keys[k], q2, NT) * (INV_ROOT * LOG2E) + jnp.concatenate(
                [b, b], axis=1
            )
            w = jnp.exp2(t - lse2)
            weights32[block(k), :] = w
            weights[block(k), :] = w.astype(BF)
        out_t = dot(values_t[...], weights[...]).astype(BF).astype(F32)
        g2_t = jnp.concatenate(
            [g2[n * TOK : (n + 1) * TOK].astype(F32).T for n in range(2)], axis=1
        )
        delta = jnp.sum(out_t * g2_t, axis=0, keepdims=True)
        for k in range(BLOCKS):
            d_prob = dot(values[k], g2, NT)
            d_scores[block(k), pl.ds(pair * 2 * TOK, 2 * TOK)] = (
                weights32[block(k), :] * (d_prob - delta)
            ).astype(BF)
        dq_t = dot(keys_t[...], d_scores[:, pl.ds(pair * 2 * TOK, 2 * TOK)]) * INV_ROOT
        for n in range(2):
            head = slice((2 * pair + n) * HEAD, (2 * pair + n + 1) * HEAD)
            out_ref[:, head] = out_t[:, n * TOK : (n + 1) * TOK].T.astype(BF)
            dq_ref[:, head] = dq_t[:, n * TOK : (n + 1) * TOK].T.astype(BF)
    rows = jnp.concatenate([pair_rows(q_ref, pair) for pair in range(PAIRS)], axis=0)
    put_partials(
        dk_refs, lambda k: (dot(d_scores[block(k), :], rows) * INV_ROOT).astype(BF)
    )


def smem():
    return pl.BlockSpec(memory_space=pltpu.SMEM)


def anywhere():
    return pl.BlockSpec(memory_space=pl.ANY)


def partial_outs(first=0):
    counts = (3, 2, 2, 2)
    shapes = [jax.ShapeDtypeStruct((n, TOK, KV), BF) for n in counts]
    return shapes, [pl.BlockSpec((n, TOK, HEAD), lambda g: (0, 0, g + first)) for n in counts]


def window_specs(rows, first=0):
    own = pl.BlockSpec((rows, HEAD), lambda g: (0, g + first))
    pair = pl.BlockSpec((2, rows, HEAD), lambda g: (0, 0, g + first))
    return [own] * 3 + [pair] * 3


def run_scores(here, docs_own, owners, queries, grads, keys, after):
    shapes, specs = partial_outs()
    wide = pl.BlockSpec((TOK, PER_GROUP * HEAD), lambda g: (0, g))
    line = pl.BlockSpec((1, TOK), lambda g: (0, 0))
    return pl.pallas_call(
        scores_kernel,
        grid=(GROUPS,),
        in_specs=[smem(), line, line, wide, wide] + window_specs(PACK) + [anywhere()],
        out_specs=[
            pl.BlockSpec((1, PER_GROUP, TOK), lambda g: (g, 0, 0)),
            pl.BlockSpec((16, 1, CAP * HQ), lambda g: (0, 0, 0)),
        ]
        + specs,
        out_shape=[
            jax.ShapeDtypeStruct((GROUPS, PER_GROUP, TOK), F32),
            jax.ShapeDtypeStruct((16, 1, CAP * HQ), F32),
        ]
        + shapes,
        scratch_shapes=[
            pltpu.VMEM((KEYS, TOK), F32),
            pltpu.VMEM((KEYS, 2 * TOK), F32),
            pltpu.VMEM((KEYS, PER_GROUP * TOK), BF),
            pltpu.VMEM((HQ, TOK), F32),
        ],
        compiler_params=pltpu.CompilerParams(
            vmem_limit_bytes=VMEM, dimension_semantics=("arbitrary",)
        ),
        cost_estimate=pl.CostEstimate(
            flops=32 << 30, bytes_accessed=6 << 20, transcendentals=2 * HQ * TOK * KEYS
        ),
        name="scores",
    )(here, docs_own, owners, queries, grads, *keys, after)


def run_grads(here, docs_own, queries, grads, lse, keys, values, first, count, begun=()):
    shapes, specs = partial_outs(first)
    wide = pl.BlockSpec((TOK, PER_GROUP * HEAD), lambda g: (0, g + first))
    return pl.pallas_call(
        grads_kernel,
        grid=(count,),
        in_specs=[
            smem(),
            pl.BlockSpec((1, TOK), lambda g: (0, 0)),
            wide,
            wide,
            pl.BlockSpec((1, PER_GROUP, TOK), lambda g: (g + first, 0, 0)),
        ]
        + window_specs(PACK, first)
        + window_specs(TOK, first)
        + [anywhere()] * len(begun),
        out_specs=[wide, wide] + specs,
        out_shape=[jax.ShapeDtypeStruct((TOK, HQ * HEAD), BF)] * 2 + shapes,
        scratch_shapes=[
            pltpu.VMEM((KEYS, TOK), F32),
            pltpu.VMEM((HEAD, KEYS), BF),
            pltpu.VMEM((HEAD, KEYS), BF),
            pltpu.VMEM((KEYS, 2 * TOK), F32),
            pltpu.VMEM((KEYS, 2 * TOK), BF),
            pltpu.VMEM((KEYS, PER_GROUP * TOK), BF),
        ],
        input_output_aliases={17 + n: n for n in range(len(begun))},
        compiler_params=pltpu.CompilerParams(
            vmem_limit_bytes=VMEM, dimension_semantics=("arbitrary",)
        ),
        cost_estimate=pl.CostEstimate(
            flops=32 << 30, bytes_accessed=8 << 20, transcendentals=HQ * TOK * KEYS
        ),
        name="grads_%d" % first,
    )(here, docs_own, queries, grads, lse, *keys, *values, *begun)


def along_z(x, step):
    return lax.ppermute(x, "ctx", [(i, i // 4 * 4 + (i + step) % 4) for i in range(16)])


def along_x(x, step):
    return lax.ppermute(x, "ctx", [(i, (i + 4 * step) % 16) for i in range(16)])


def along_y(x, step):
    return lax.ppermute(x, "dp", [(i, (i + 2 * step) % 8) for i in range(8)])


def other_core(x):
    return lax.ppermute(x, "dp", [(i, i ^ 1) for i in range(8)])


def pick_kernel(z_ref, own, row_1, row_2, *outs):
    for e, out in zip((1, 2, 3), outs):
        wrapped = z_ref[0] + e > 3
        out[0] = jnp.where(wrapped, row_1[...], own[...])
        out[1] = jnp.where(wrapped, row_2[...], row_1[...])


def for_peers(own, z):
    blocks = [own, along_x(own, 1), along_x(own, 2)]
    pairs = small_call(
        pick_kernel, [smem()] + in_vmem(3), [((2, *own.shape), BF)] * 3, "pick", 1
    )(z, *blocks)
    return blocks, list(pairs)


def to_peers(pairs):
    return [along_z(pair, e) for e, pair in zip((1, 2, 3), pairs)]


def across(x, axis_step):
    return lax.ppermute(x, "ctx", [(i, i ^ axis_step) for i in range(16)])


def swap_sum(x, axis_step, after=()):
    (total,) = small_call(
        swap_sum_kernel,
        in_vmem(2) + [anywhere()] * len(after),
        [(x.shape, BF)],
        "swap_sum",
        1,
    )(x, across(x, axis_step), *after)
    return total


def swap_sum_kernel(own, got, *refs):
    refs[-1][...] = (own[...].astype(F32) + got[...].astype(F32)).astype(BF)


def in_vmem(count):
    return [pl.BlockSpec(memory_space=pltpu.VMEM)] * count


def small_call(kernel, specs, shapes, name, us, scratch=(), grid=()):
    return pl.pallas_call(
        kernel,
        grid=grid,
        in_specs=specs,
        out_specs=in_vmem(len(shapes)),
        out_shape=[jax.ShapeDtypeStruct(shape, dtype) for shape, dtype in shapes],
        scratch_shapes=list(scratch),
        compiler_params=pltpu.CompilerParams(vmem_limit_bytes=SMALL_VMEM),
        cost_estimate=pl.CostEstimate(
            flops=us << 30, bytes_accessed=us << 21, transcendentals=0
        ),
        name=name,
    )


def pack_kernel(keys, docs, out):
    out[0:TOK, :] = keys[...]
    rows = jnp.broadcast_to(docs[...].astype(F32), (DOC_ROWS, TOK)).astype(BF)
    for group in range(GROUPS):
        out[TOK:PACK, group * HEAD : (group + 1) * HEAD] = rows


def gate_kernel(*refs):
    pass


def gate(arrays, after):
    return pl.pallas_call(
        gate_kernel,
        in_specs=[anywhere()] * (len(arrays) + 1),
        out_specs=[anywhere()] * len(arrays),
        out_shape=[jax.ShapeDtypeStruct(array.shape, array.dtype) for array in arrays],
        input_output_aliases={n: n for n in range(len(arrays))},
        name="gate",
    )(*arrays, after)


def sum_terms(terms):
    total = terms[0][...].astype(F32)
    for term in terms[1:]:
        total = total + term[...].astype(F32)
    return total.astype(BF)


def key_grad_kernel(*refs):
    refs[-1][...] = sum_terms(refs[:-1])


def row_sums_kernel(z_ref, own, *refs):
    *got, _after, here_out, near_out, far_out = refs
    here_row, row_1, row_2 = (own[n].astype(F32) for n in range(3))
    for n, pair in enumerate(got):
        before = z_ref[0] + 1 + n > 3
        near, far = pair[0].astype(F32), pair[1].astype(F32)
        here_row = here_row + jnp.where(before, 0.0, near)
        row_1 = row_1 + jnp.where(before, near, far)
        row_2 = row_2 + jnp.where(before, far, 0.0)
    here_out[...] = here_row
    near_out[...] = row_1.astype(BF)
    far_out[...] = row_2.astype(BF)


def sum_kernel(*refs):
    refs[-1][...] = sum_terms(refs[:4])


def adapter_kernel(core_ref, *refs):
    up, low_rank, rows, _after, grad_out, middle_out, keep_out, send_out = refs[3:]
    grad = sum_terms(refs[:3])
    grad_out[...] = grad
    middle = (ADAPTER_SCALE * dot(grad, up[...], NT)).astype(BF)
    middle_out[...] = middle
    middle_t = middle.astype(F32).T.astype(BF)
    low_rank_t = low_rank[...].astype(F32).T.astype(BF)
    half = keep_out.shape[0]
    model = rows.shape[1]
    first = core_ref[0] == 0

    def split(part, columns):
        low, high = part[:half].astype(BF), part[half:].astype(BF)
        keep_out[:, columns] = jnp.where(first, low, high)
        send_out[:, columns] = jnp.where(first, high, low)

    step = 1024
    for n in range(model // step):
        columns = slice(n * step, (n + 1) * step)
        split(dot(middle_t, rows[:, columns]), columns)
    split(ADAPTER_SCALE * dot(low_rank_t, grad), slice(model, model + KV))


def quarters_kernel(y_ref, keep, got, mine_out, *send_outs):
    part = mine_out.shape[1]
    for e, out in enumerate((mine_out,) + send_outs):
        first = lax.rem(y_ref[0] + e, 4) * part
        columns = pl.ds(pl.multiple_of(first, HEAD), part)
        out[...] = (keep[:, columns].astype(F32) + got[:, columns].astype(F32)).astype(BF)


def assemble_kernel(y_ref, *refs):
    *parts, _d_key, _slots, out = refs
    width = parts[0].shape[1]
    for e, part in enumerate(parts):
        first = lax.rem(y_ref[0] + 4 - e, 4) * width
        out[:, pl.ds(pl.multiple_of(first, HEAD), width)] = part[...]


def totals_kernel(core_ref, mine, other, down_out, up_out):
    half = mine.shape[0]
    model = down_out.shape[1]
    first = core_ref[0] == 0
    step = 512

    def whole(columns):
        a, b = mine[:, columns].astype(F32), other[:, columns].astype(F32)
        return jnp.concatenate([jnp.where(first, a, b), jnp.where(first, b, a)], axis=0)

    for n in range(model // step):
        columns = slice(n * step, (n + 1) * step)
        down_out[:, columns] = whole(columns)
    up_out[...] = whole(slice(model, model + KV))


def slots_kernel(got, out, rows):
    for slot in range(CAP):
        rows[pl.ds(slot, got.shape[0], stride=CAP), 0:HQ] = got[:, 0, slot * HQ : (slot + 1) * HQ]
    out[...] = rows[...].T[:HQ]


def sum_home(parts, z, after):
    got = [along_z(part, -distance) for distance, part in zip((3, 2, 1), parts[1:])]
    here_row, near, far = small_call(
        row_sums_kernel,
        [smem()] + in_vmem(4) + [anywhere()],
        [((TOK, KV), F32), ((TOK, KV), BF), ((TOK, KV), BF)],
        "row_sums",
        1,
    )(z, parts[0], *got[::-1], after)
    return here_row, along_x(near, -1), along_x(far, -2)


def local(
    normed,
    queries,
    rotated_keys,
    value_weight,
    adapter_down,
    adapter_up,
    attention_cotangent,
    document_index,
    owner_routing,
):
    ctx = lax.axis_index("ctx")
    dp = lax.axis_index("dp")
    y, core = dp // 2, dp % 2
    rows = normed[0]
    low_rank = dot(rows, adapter_down).astype(BF)
    values = (dot(rows, value_weight) + ADAPTER_SCALE * dot(low_rank, adapter_up)).astype(BF)
    z = (ctx % 4).reshape(1)
    (packed,) = small_call(pack_kernel, in_vmem(2), [((PACK, KV), BF)], "pack", 1)(
        rotated_keys[0], document_index
    )
    key_own, key_pairs = for_peers(packed, z)
    key_parts = key_own + to_peers(key_pairs)
    (values,) = gate([values], key_own[1])
    value_own, value_pairs = for_peers(values, z)
    value_parts = value_own + to_peers(value_pairs)
    here, y, core = (n.reshape(1) for n in (ctx, y, core))
    lse, own_lse, *dv_parts = run_scores(
        here,
        document_index,
        owner_routing.reshape(1, TOK),
        queries[0],
        attention_cotangent[0],
        key_parts,
        value_pairs[0],
    )
    args = (here, document_index, queries[0], attention_cotangent[0], lse, key_parts, value_parts)
    half_done = run_grads(*args, 0, GROUPS // 2)
    out, dq, *dk_parts = run_grads(*args, GROUPS // 2, GROUPS - GROUPS // 2, half_done)

    peers = lax.axis_size("ctx")
    got_lse = lax.all_to_all(own_lse, "ctx", split_axis=0, concat_axis=0, tiled=True)
    (lse_rows,) = small_call(
        slots_kernel,
        in_vmem(1),
        [((HQ, peers * CAP), F32)],
        "slots",
        1,
        [pltpu.VMEM((peers * CAP, TOK), F32)],
    )(got_lse)

    dv_terms = sum_home(dv_parts, z, half_done[1])

    rank, model = adapter_up.shape[0], rows.shape[1]
    half, width = rank // 2, model + KV
    part = width // 4
    value_grad, middle, keep, send = small_call(
        adapter_kernel,
        [smem()] + in_vmem(6) + [anywhere()],
        [((TOK, KV), BF), ((TOK, rank), BF), ((half, width), BF), ((half, width), BF)],
        "adapter",
        3,
    )(core, *dv_terms, adapter_up, low_rank, rows, dq)
    mine, *sends = small_call(
        quarters_kernel, [smem()] + in_vmem(2), [((half, part), BF)] * 4, "quarters", 1
    )(y, keep, other_core(send))
    normed_input_gradient = (
        dot(value_grad, value_weight, NT) + dot(middle, adapter_down, NT)
    ).astype(BF)
    (mine,) = small_call(
        sum_kernel, in_vmem(4) + [anywhere()], [((half, part), BF)], "y_sum", 1
    )(mine, *[along_y(send, e) for e, send in zip((1, 2, 3), sends)], normed_input_gradient)
    dk_parts[1:] = gate(dk_parts[1:], mine)
    dk_terms = sum_home(dk_parts, z, here)
    (d_key,) = small_call(key_grad_kernel, in_vmem(3), [((TOK, KV), BF)], "key_grad", 1)(*dk_terms)
    for axis_step, after in ((4, ()), (8, ()), (1, (dk_terms[0],)), (2, (lse_rows,))):
        mine = swap_sum(mine, axis_step, after)
    (whole,) = small_call(
        assemble_kernel,
        [smem()] + in_vmem(4) + [anywhere()] * 2,
        [((half, width), BF)],
        "assemble",
        1,
    )(y, mine, *[along_y(mine, e) for e in (1, 2, 3)], d_key, lse_rows)
    total_down, total_up = small_call(
        totals_kernel, [smem()] + in_vmem(2), [((rank, model), F32), ((rank, KV), F32)], "totals", 2
    )(core, whole, other_core(whole))

    return (
        out[None],
        dq[None],
        d_key[None],
        normed_input_gradient[None],
        total_down.T,
        total_up,
        lse_rows.T[None],
    )


def solution(mesh):
    tokens = P("dp", "ctx", None)
    return jax.shard_map(
        local,
        mesh=mesh,
        in_specs=(tokens, tokens, tokens, P(), P(), P(), tokens, P("dp", "ctx"), tokens),
        out_specs=(tokens, tokens, tokens, tokens, P(), P(), tokens),
        check_vma=False,
    )
```
